256 devices in a mesh: dp: 32 (over x, z), tensor: 8 (over y, core).
Axes of the slice: x: 4, y: 4, z: 8, core: 2. Of those that a mesh axis runs over, the one named last changes fastest.
Arguments:
- token_rows: bfloat16 [16384, 8192], P(('dp', 'tensor')), may hold values from -24 to 24
- advantage: int32 [16384], P(('dp', 'tensor')), may hold values from 1 to 81920
- cotangent: bfloat16 [16384, 2048], P('dp', 'tensor'), may hold values from -1 to 1
- master: float32 [8192, 2048], P('dp', 'tensor'), may hold values from -3 to 3
- moment_one: float32 [8192, 2048], P('dp', 'tensor'), may hold values from -3 to 3
- moment_two: float32 [8192, 2048], P('dp', 'tensor'), may hold values from 0.1 to 3
Outputs:
- weights: bfloat16 [8192, 2048], P(None, 'tensor')
- new_master: float32 [8192, 2048], P('dp', 'tensor')
- new_moment_one: float32 [8192, 2048], P('dp', 'tensor')
- new_moment_two: float32 [8192, 2048], P('dp', 'tensor')
The draws below stay inside these ranges and needn't reach their ends.
Inputs may be any that keep to these rules, and one draw needn't show every extreme that they name: advantage weight in units of 2**-12.
All inputs are finite; a program needn't handle non-finite values.
Results may differ from the reference program's by a relative error of at most 0.00042.
Values may be sent and summed in bfloat16 or wider, within the bound.
No kernel may reach another device: no remote copies, remote signals or barrier semaphores. Data moves between devices by JAX's collectives and lax.ppermute only.
A program may use at most 64 MiB of HBM per device.

```python
import math
import jax
import jax.numpy as jnp

D = 8192
COLS = 2048
STEP = 10
TOK_REP = 512
TOKENS = 16384
N_DP = 32


def draw_token_rows(key, part):
    key = jax.random.fold_in(key, 11)
    key_common, key_single, key_scale = jax.random.split(key, 3)
    copies = TOKENS // TOK_REP
    feature_scale = jnp.exp(jax.random.uniform(key_scale, (1, D), jnp.float32, jnp.log(0.3), jnp.log(3.0)))
    position = jnp.arange(D, dtype=jnp.float32)[None, :] / (D - 1)
    common = jnp.clip(jax.random.normal(key_common, (TOK_REP, D), jnp.float32), -4.0, 4.0)
    single = jnp.clip(jax.random.normal(key_single, (TOKENS, D), jnp.float32), -4.0, 4.0)
    shared_part = 1.8 - 1.6 * position
    single_part = 0.2 + 1.6 * position
    repeated = jnp.tile(common, (copies, 1))
    values = (shared_part * repeated + single_part * single) * feature_scale
    return values.astype(jnp.bfloat16)


def draw_cotangent(key, part):
    key = jax.random.fold_in(key, 7)
    key_common, key_single, key_rows, key_cols = jax.random.split(key, 4)
    copies = TOKENS // TOK_REP
    column_scale = jnp.exp(jax.random.uniform(key_cols, (1, COLS), jnp.float32) * jnp.log(10.0))
    row_scale = jnp.exp(jax.random.uniform(key_rows, (TOK_REP, 1), jnp.float32) * jnp.log(10.0))
    common = jnp.clip(jax.random.normal(key_common, (TOK_REP, COLS), jnp.float32), -4.0, 4.0)
    single = jnp.clip(jax.random.normal(key_single, (TOKENS, COLS), jnp.float32), -4.0, 4.0)
    shared_part = 1.2
    single_part = 0.8
    amplitude = 0.0012
    repeated = jnp.tile(common, (copies, 1))
    scales = jnp.tile(row_scale, (copies, 1)) * column_scale
    values = amplitude * (shared_part * repeated + single_part * single) * scales
    return values.astype(jnp.bfloat16)


def touch_ends(entries, stream_key, low, top_value):
    dims = entries.shape
    spot = [jax.random.randint(jax.random.fold_in(stream_key, axis), (), 0, dims[axis]) for axis in range(len(dims))]
    entries = entries.at[tuple(spot)].set(low)
    longest = dims.index(max(dims))
    spot[longest] = (spot[longest] + 1) % dims[longest]
    return entries.at[tuple(spot)].set(top_value)


def level_of(rng, shape, cuts, smallest, high):
    gain = 1.0
    for dim, shards_of in cuts:
        steps = jax.random.uniform(jax.random.fold_in(jax.random.fold_in(rng, 6), dim), (shards_of,), jnp.float32, smallest / len(cuts), high / len(cuts))
        gain = gain * jnp.repeat(jnp.exp(steps), shape[dim] // shards_of).reshape((-1,) + (1,) * (len(shape) - 1 - dim))
    return gain


def noise(rng, shape, spread, most, cuts=(), held_as=jnp.bfloat16):
    factor_of = level_of(rng, shape, cuts, -0.22, 0.18) if cuts else 1.0
    entries = jax.random.normal(rng, shape, jnp.float32) * spread * factor_of
    return jnp.minimum(jnp.maximum(entries, -most), most).astype(held_as)


def setup_inputs(seed: int = 0) -> dict:
    key_of = jax.random.split(jax.random.key(seed), 7)
    return {
        "token_rows": draw_token_rows(jax.random.fold_in(key_of[6], 71), 0),
        "advantage": touch_ends(jax.random.randint(key_of[1], (TOKENS,), 1, 81921), jax.random.fold_in(key_of[1], 1), 1, 81920).astype(jnp.int32),
        "cotangent": draw_cotangent(jax.random.fold_in(key_of[6], 71), 0),
        "master": noise(key_of[3], (D, COLS), 0.5, 3.0, ((0, 32), (1, 8)), jnp.float32),
        "moment_one": noise(key_of[4], (D, COLS), 0.5, 3.0, ((0, 32), (1, 8)), jnp.float32),
        "moment_two": jnp.clip(jnp.exp(math.log(3.0) - 3.4011974 * jax.random.uniform(key_of[5], (D, COLS), jnp.float32) ** level_of(key_of[5], (D, COLS), ((0, 32), (1, 8)), -0.2, 0.2)), 0.1, 3.0),
    }


SCALE_FIXED = 2.0 ** (-12)
EPS_ADA = 1e-06

def adasum(first, second):
    cross = jnp.sum(first * second)
    first_sq = jnp.sum(first * first)
    second_sq = jnp.sum(second * second)
    return (1.0 - cross / (2.0 * first_sq + EPS_ADA)) * first + (1.0 - cross / (2.0 * second_sq + EPS_ADA)) * second

def replica_grad(token_rows, advantage, cotangent, replica):
    start = replica * TOK_REP
    rows = token_rows[start:start + TOK_REP]
    weights = advantage[start:start + TOK_REP].astype(jnp.float32) * SCALE_FIXED
    mean_weight = jnp.sum(weights) / TOK_REP
    weighted = (weights[:, None] * cotangent[start:start + TOK_REP].astype(jnp.float32)).astype(jnp.bfloat16)
    return jnp.dot(rows.T, weighted, preferred_element_type=jnp.float32) / mean_weight

def reference(token_rows, advantage, cotangent, master, moment_one, moment_two):

    def tree(members):
        if len(members) == 1:
            return replica_grad(token_rows, advantage, cotangent, members[0])
        return adasum(tree(members[0::2]), tree(members[1::2]))
    combined = tree(list(range(N_DP)))
    new_one = 0.9 * moment_one + 0.1 * combined
    new_two = 0.95 * moment_two + 0.05 * combined * combined
    first_hat = new_one / (1.0 - 0.9 ** STEP)
    second_hat = new_two / (1.0 - 0.95 ** STEP)
    updated = master - 0.001 * (first_hat / (jnp.sqrt(second_hat) + 1e-08) + 0.1 * master)
    return (updated.astype(jnp.bfloat16), updated, new_one, new_two)
```

```python
import functools
import jax
import jax.numpy as jnp
from jax import lax
from jax.experimental import pallas as pl
from jax.experimental.pallas import tpu as pltpu
from jax.sharding import Mesh, PartitionSpec as P

STEP = 10
SCALE_FIXED = 2.0 ** (-12)
EPS_ADA = 1e-06

NX, NZ, NY, NC = 4, 8, 4, 2
REP = NX * NZ
TOK = 512
BLK = 256
ROWS_A = 288
F32 = jnp.float32
BF16 = jnp.bfloat16
HIGH = lax.Precision.HIGHEST


def shift(array, axis, size, by):
    return lax.ppermute(array, axis, [(i, (i + by) % size) for i in range(size)])


def ring(block, axis, size):
    found = {0: [block]}
    fwd = bwd = block
    half = size // 2
    for k in range(1, half):
        fwd, bwd = shift(fwd, axis, size, 1), shift(bwd, axis, size, -1)
        found[k], found[size - k] = [fwd], [bwd]
    cut = block.shape[0] // 2
    found[half] = [shift(fwd[:cut], axis, size, 1), shift(bwd[cut:], axis, size, -1)]
    return found


def whole(pieces):
    return pieces[0] if len(pieces) == 1 else jnp.concatenate(pieces, axis=0)


def gather_plane(block, cut):
    first, second = block[:cut][None], block[cut:][None]
    out = []
    if cut:
        line = ring_rows(first, "z", NZ)
        for kx, pieces in ring(line, "x", NX).items():
            at = 0
            for piece in pieces:
                out.append((piece, 0, [(kx, kz) for kz in range(at, at + piece.shape[0])]))
                at += piece.shape[0]
    if cut < block.shape[0]:
        line = ring_rows(second, "x", NX)
        for kz, pieces in ring(line, "z", NZ).items():
            at = 0
            for piece in pieces:
                out.append((piece, cut, [(kx, kz) for kx in range(at, at + piece.shape[0])]))
                at += piece.shape[0]
    return out


def ring_rows(block, axis, size):
    rows = block.shape[1]
    found = ring(block[0], axis, size)
    return jnp.stack([whole(found[k]) for k in range(size)])


def replica_of(place, kx, kz):
    return lax.rem(place[0] - kx + NX, NX) * NZ + lax.rem(place[1] - kz + NZ, NZ)


def grads_kernel(layout, place, x_hbm, *refs):
    count = len(layout)
    pieces, (mean_ref, g_hbm, sums_ref) = refs[:count], refs[count:count + 3]
    xv, wv, gv, xsem, wsem, gsem = refs[count + 3:]
    order = [(kx, kz) for kx in range(NX) for kz in range(NZ)]
    copies = {}
    for slot, (kx, kz) in enumerate(order):
        r = replica_of(place, kx, kz)
        mine = [pltpu.make_async_copy(x_hbm.at[:, r], xv.at[r], xsem.at[slot])]
        for no, (offset, rows, keys) in enumerate(layout):
            if (kx, kz) in keys:
                mine.append(pltpu.make_async_copy(
                    pieces[no].at[keys.index((kx, kz))], wv.at[r, pl.ds(offset, rows)],
                    wsem.at[slot, int(offset > 0)]))
        for copy in mine:
            copy.start()
        copies[slot] = mine
    outs = []
    for slot, (kx, kz) in enumerate(order):
        r = replica_of(place, kx, kz)
        for copy in copies[slot]:
            copy.wait()
        rows = xv[r].reshape(TOK, BLK)
        gv[r] = lax.dot_general(rows, wv[r], (((0,), (0,)), ((), ())), preferred_element_type=F32)
        out = pltpu.make_async_copy(gv.at[r], g_hbm.at[r], gsem.at[slot])
        out.start()
        outs.append(out)

    def add(j, total):
        y = gv[:, pl.ds(pl.multiple_of(j * 8, 8), 8), :].reshape(BLK, BLK)
        high = y.astype(BF16)
        low = (y - high.astype(F32)).astype(BF16)
        both = jnp.concatenate([high, low], axis=0)
        return total + lax.dot_general(high, both, (((1,), (1,)), ((), ())), preferred_element_type=F32)

    total = lax.fori_loop(0, BLK // 8, add, jnp.zeros((BLK, 2 * BLK), F32))
    cross = total[:, BLK:]
    total = total[:, :BLK] + cross + cross.T
    i = lax.broadcasted_iota(jnp.int32, (BLK, BLK), 0)
    j = lax.broadcasted_iota(jnp.int32, (BLK, BLK), 1)
    total = jnp.where(i % 8 == j % 8, total, 0.0)
    pick_rows = (lax.broadcasted_iota(jnp.int32, (REP, BLK), 0)
                 == lax.broadcasted_iota(jnp.int32, (REP, BLK), 1) // 8).astype(F32)
    pick_cols = (lax.broadcasted_iota(jnp.int32, (BLK, 128), 1) % REP
                 == lax.broadcasted_iota(jnp.int32, (BLK, 128), 0) // 8).astype(F32)
    gram = jnp.dot(jnp.dot(pick_rows, total, preferred_element_type=F32, precision=HIGH), pick_cols,
                   preferred_element_type=F32, precision=HIGH)
    sums_ref[0:REP] = gram
    lane = lax.broadcasted_iota(jnp.int32, (8, 128), 1)
    mine = replica_of(place, 0, 0)
    sums_ref[REP:REP + 8] = jnp.where(lane % REP == mine, mean_ref[...], 0.0)
    for out in outs:
        out.wait()


def grads_and_sums(place, rows, pieces, mean):
    layout = [(offset, piece.shape[1], keys) for piece, offset, keys in pieces]
    any_spec = pl.BlockSpec(memory_space=pl.ANY)
    return pl.pallas_call(
        functools.partial(grads_kernel, layout),
        out_shape=(jax.ShapeDtypeStruct((REP, BLK, BLK), F32), jax.ShapeDtypeStruct((REP + 8, 128), F32)),
        in_specs=[pl.BlockSpec(memory_space=pltpu.SMEM), any_spec] + [any_spec] * len(layout)
        + [pl.BlockSpec(memory_space=pltpu.VMEM)],
        out_specs=(any_spec, pl.BlockSpec(memory_space=pltpu.VMEM)),
        scratch_shapes=[
            pltpu.VMEM((REP, NY * NC, TOK // (NY * NC), BLK), BF16),
            pltpu.VMEM((REP, TOK, BLK), BF16),
            pltpu.VMEM((REP, BLK, BLK), F32),
            pltpu.SemaphoreType.DMA((REP,)),
            pltpu.SemaphoreType.DMA((REP, 2)),
            pltpu.SemaphoreType.DMA((REP,)),
        ],
        compiler_params=pltpu.CompilerParams(vmem_limit_bytes=48 * 2**20),
        cost_estimate=pl.CostEstimate(flops=6 * 10**9, bytes_accessed=24 * 2**20, transcendentals=0),
    )(place, rows, *[piece for piece, _, _ in pieces], mean)


def tree_weights(sums):
    lane = lax.broadcasted_iota(jnp.int32, (REP, 128), 1) % REP
    row = lax.broadcasted_iota(jnp.int32, (REP, 128), 0)
    inverse_lanes = (float(NY * NC) / sums[REP:REP + 1])
    inverse_rows = jnp.sum(jnp.where((lax.broadcasted_iota(jnp.int32, (REP, 128), 1) == row),
                                     jnp.broadcast_to(inverse_lanes, (REP, 128)), 0.0), axis=1, keepdims=True)
    table = sums[0:REP] * inverse_rows * inverse_lanes
    factor = inverse_rows
    first = lax.broadcasted_iota(jnp.int32, (REP, 128), 1) < REP
    size = REP
    while size > 1:
        half = size // 2
        own = lane == row
        other_rows = lane == (row + half) % REP
        other_lanes = row == (lane + half) % REP
        own_r = jnp.sum(jnp.where(own & first, table, 0.0), axis=1, keepdims=True)
        cross_r = jnp.sum(jnp.where(other_rows & first, table, 0.0), axis=1, keepdims=True)
        own_l = jnp.sum(jnp.where(own, table, 0.0), axis=0, keepdims=True)
        cross_l = jnp.sum(jnp.where(other_lanes, table, 0.0), axis=0, keepdims=True)
        coef_r = 1.0 - cross_r / (2.0 * own_r + EPS_ADA)
        coef_l = 1.0 - cross_l / (2.0 * own_l + EPS_ADA)
        factor = factor * coef_r
        table = table * coef_r * coef_l
        table = table + pltpu.roll(table, half, 0)
        table = table + pltpu.roll(table, half, 1)
        size = half
    return jnp.broadcast_to(factor, (REP, 128))


def update_kernel(sums_ref, g_hbm, master_ref, one_ref, two_ref, weights_ref, master_out, one_out, two_out,
                  gv, factors, sem):
    copies = [pltpu.make_async_copy(g_hbm.at[r], gv.at[r], sem.at[r]) for r in range(REP)]
    for copy in copies:
        copy.start()
    factors[...] = tree_weights(sums_ref[...])
    for copy in copies:
        copy.wait()

    def strip(s, _):
        at = pl.ds(pl.multiple_of(s * 16, 16), 16)
        combined = jnp.zeros((16, BLK), F32)
        for r in range(REP):
            scale = factors[r:r + 1, :]
            combined = combined + jnp.concatenate([scale, scale], axis=1) * gv[r, at, :]
        new_one = 0.9 * one_ref[at, :] + 0.1 * combined
        new_two = 0.95 * two_ref[at, :] + 0.05 * combined * combined
        first_hat = new_one / (1.0 - 0.9**STEP)
        second_hat = new_two / (1.0 - 0.95**STEP)
        master = master_ref[at, :]
        updated = master - 0.001 * (first_hat / (jnp.sqrt(second_hat) + 1e-08) + 0.1 * master)
        weights_ref[at, :] = updated.astype(BF16)
        master_out[at, :] = updated
        one_out[at, :] = new_one
        two_out[at, :] = new_two
        return 0

    lax.fori_loop(0, BLK // 16, strip, 0)


def update(sums, grads, master, one, two):
    vmem = pl.BlockSpec(memory_space=pltpu.VMEM)
    state = jax.ShapeDtypeStruct((BLK, BLK), F32)
    return pl.pallas_call(
        update_kernel,
        out_shape=(jax.ShapeDtypeStruct((BLK, BLK), BF16), state, state, state),
        in_specs=[vmem, pl.BlockSpec(memory_space=pl.ANY), vmem, vmem, vmem],
        out_specs=(vmem,) * 4,
        scratch_shapes=[
            pltpu.VMEM((REP, BLK, BLK), F32),
            pltpu.VMEM((REP, 128), F32),
            pltpu.SemaphoreType.DMA((REP,)),
        ],
        compiler_params=pltpu.CompilerParams(vmem_limit_bytes=32 * 2**20),
        cost_estimate=pl.CostEstimate(flops=5 * 10**6, bytes_accessed=10 * 2**20, transcendentals=0),
    )(sums, grads, master, one, two)


def place_kernel(layout, place, *refs):
    count = len(layout)
    pieces, out_hbm, sem = refs[:count], refs[count], refs[count + 1]
    copies = []
    for no, (offset, rows, keys) in enumerate(layout):
        for index, (kx, kz) in enumerate(keys):
            r = replica_of(place, kx, kz)
            copies.append(pltpu.make_async_copy(
                pieces[no].at[index], out_hbm.at[r, pl.ds(offset, rows)], sem.at[len(copies)]))
    for copy in copies:
        copy.start()
    for copy in copies:
        copy.wait()


def place_rows(place, pieces):
    layout = [(offset, piece.shape[1], keys) for piece, offset, keys in pieces]
    any_spec = pl.BlockSpec(memory_space=pl.ANY)
    total = sum(len(keys) for _, _, keys in layout)
    return pl.pallas_call(
        functools.partial(place_kernel, layout),
        out_shape=jax.ShapeDtypeStruct((REP, BLK, BLK), BF16),
        in_specs=[pl.BlockSpec(memory_space=pltpu.SMEM)] + [any_spec] * len(layout),
        out_specs=any_spec,
        scratch_shapes=[pltpu.SemaphoreType.DMA((total,))],
        cost_estimate=pl.CostEstimate(flops=0, bytes_accessed=8 * 2**20, transcendentals=0),
    )(place, *[piece for piece, _, _ in pieces])


def gather_advantage(advantage):
    core, y = lax.axis_index("c"), lax.axis_index("y")
    other = shift(advantage, "c", NC, 1)
    pair = jnp.where(core == 0, jnp.concatenate([advantage, other]), jnp.concatenate([other, advantage]))
    parts = [pair] + [shift(pair, "y", NY, -k) for k in range(1, NY)]
    turned = jnp.concatenate(parts + parts)
    return lax.dynamic_slice_in_dim(turned, (NY - y) * pair.shape[0], TOK)


def total_over_slice(sums):
    for axis, size in (("c", NC), ("y", NY), ("x", NX), ("z", NZ)):
        stride = 1
        while stride < size:
            sums = sums + lax.ppermute(sums, axis, [(i, i ^ stride) for i in range(size)])
            stride *= 2
    return sums


def local(token_rows, advantage, cotangent, master, moment_one, moment_two):
    place = jnp.stack([lax.axis_index("x"), lax.axis_index("z")]).astype(jnp.int32)
    blocks = lax.all_to_all(token_rows, ("x", "z"), 1, 0, tiled=True)
    rows = lax.all_gather(blocks, ("y", "c"), axis=0, tiled=True)
    rows = rows.reshape(NY * NC, REP, TOK // (NY * NC), BLK)
    weights = gather_advantage(advantage).astype(F32) * SCALE_FIXED
    weighted = (weights[:, None] * cotangent.astype(F32)).astype(BF16)
    mean = jnp.full((8, 128), jnp.sum(weights) / TOK)
    grads, sums = grads_and_sums(place, rows, gather_plane(weighted, ROWS_A), mean)
    sums = total_over_slice(sums)
    new_weights, new_master, new_one, new_two = update(sums, grads, master, moment_one, moment_two)
    out = place_rows(place, gather_plane(new_weights, 128))
    return (out.reshape(REP * BLK, BLK), new_master, new_one, new_two)


def solution(mesh):
    fine = Mesh(mesh.devices.reshape(NX, NZ, NY, NC), ("x", "z", "y", "c"))
    dp, tensor = ("x", "z"), ("y", "c")
    state = P(dp, tensor)
    return jax.shard_map(
        local,
        mesh=fine,
        in_specs=(P(dp + tensor, None), P(dp + tensor), state, state, state, state),
        out_specs=(P(None, tensor), state, state, state),
        check_vma=False,
    )
```

```python
import functools
import jax
import jax.numpy as jnp
from jax import lax
from jax.experimental import pallas as pl
from jax.experimental.pallas import tpu as pltpu
from jax.sharding import Mesh, PartitionSpec as P

STEP = 10
SCALE_FIXED = 2.0 ** (-12)
EPS_ADA = 1e-06

NX, NZ, NY, NC = 4, 8, 4, 2
REP = NX * NZ
TOK = 512
BLK = 256
ROWS_A = 288
F32 = jnp.float32
BF16 = jnp.bfloat16
HIGH = lax.Precision.HIGHEST


def shift(array, axis, size, by):
    return lax.ppermute(array, axis, [(i, (i + by) % size) for i in range(size)])


def side(at, core):
    return 1 - 2 * ((at + core) % 2)


def near(array, axis, size, which):
    pairs = [(a * NC + c, (a + which * side(a, c)) % size * NC + c) for a in range(size) for c in range(NC)]
    return lax.ppermute(array, (axis, "c"), pairs)


def swapped_ring(block, axis, size):
    pair = jnp.stack([block, near(block, axis, size, 1)])
    found, held, which = [pair], pair, -1
    for _ in range(size // 2 - 1):
        held = near(held, axis, size, which)
        found.append(held)
        which = -which
    return found


def gather_plane(block, cut):
    line = jnp.concatenate(swapped_ring(block[:cut], "z", NZ))
    other = jnp.concatenate(swapped_ring(block[cut:], "x", NX))
    ahead = near(line, "x", NX, 1)
    behind = near(line, "x", NX, -1)
    far = near(ahead, "x", NX, -1)
    out = [(piece, 0, [((), kx, 1, 0, NZ)]) for kx, piece in enumerate((line, ahead, behind, far))]
    for no, piece in enumerate(swapped_ring(other, "z", NZ)):
        out.append((piece, cut, [((i,), 0, NX, 2 * no + i, 1) for i in range(2)]))
    return out


STEPS = (0, 1, -1, -2, 2, 3, -3, -4)


def replica_of(place, kx, kz):
    x = lax.rem(place[0] + place[2] * STEPS[kx] + NX, NX)
    z = lax.rem(place[1] + place[3] * STEPS[kz] + NZ, NZ)
    return x * NZ + z


def mirrored(k, size):
    return jnp.where((k == 0) | (k == size - 1), k, k + 1 - 2 * ((k + 1) % 2))


def replicas_of(place, slots):
    def step(k):
        return sum(jnp.where(k == i, STEPS[i], 0) for i in range(NZ))

    x = lax.rem(place[0] + place[2] * step(slots // NZ) + NX, NX)
    z = lax.rem(place[1] + place[3] * step(slots % NZ) + NZ, NZ)
    return x * NZ + z


def grads_kernel(layout, place, *refs):
    tokens = NY * NC
    x_pieces, refs = refs[:tokens], refs[tokens:]
    count = len(layout)
    pieces, (mean_ref, g_hbm, sums_ref) = refs[:count], refs[count:count + 3]
    xv, wv, gv, xsem, wsem, gsem = refs[count + 3:]
    y, core, turn = place[4], place[5], place[6]
    parts, across, along = [], [], [[] for _ in range(NX)]
    for no in range(tokens):
        c = core if no < NY else 1 - core
        row = lax.rem(y + (turn if no < NY else -turn) * STEPS[no % NY] + NY, NY)
        parts.append(pltpu.make_async_copy(x_pieces[no], xv.at[row, c], xsem.at[no]))
    for no, (offset, rows, chunks) in enumerate(layout):
        for chunk, (index, kx, nx, kz, nz) in enumerate(chunks):
            source = pieces[no].at[index] if index else pieces[no]
            copy = pltpu.make_async_copy(
                source.reshape(nx, nz, rows, BLK),
                wv.at[pl.ds(kx, nx), pl.ds(kz, nz), pl.ds(offset, rows)], wsem.at[no, chunk])
            (across if offset else along[kx]).append(copy)
    for copy in parts + across + sum(along, []):
        copy.start()
    for copy in parts + across:
        copy.wait()

    def multiply(slot, _):
        kx, kz = slot // NZ, lax.rem(slot, NZ)
        other = mirrored(kx, NX) * NZ + mirrored(kz, NZ)
        rows = jnp.stack([xv[:, 0, jnp.where(core == 0, slot, other)],
                          xv[:, 1, jnp.where(core == 0, other, slot)]], axis=1).reshape(TOK, BLK)
        gv[slot] = lax.dot_general(rows, wv[kx, kz], (((0,), (0,)), ((), ())), preferred_element_type=F32)
        return 0

    outs = []
    for part in range(NX):
        for copy in along[part]:
            copy.wait()
        lax.fori_loop(part * NZ, (part + 1) * NZ, multiply, 0, unroll=2)
        at = pl.ds(part * NZ, NZ)
        outs.append(pltpu.make_async_copy(gv.at[at], g_hbm.at[at], gsem.at[part]))
        outs[-1].start()

    def add(j, total):
        y = jnp.concatenate(
            [gv[:, pl.ds(pl.multiple_of(j * 32 + 8 * h, 8), 8), :].reshape(BLK, BLK) for h in range(4)], axis=1)
        high = y.astype(BF16)
        low = (y - high.astype(F32)).astype(BF16)
        both = jnp.concatenate([high, low], axis=0)
        return total + lax.dot_general(high, both, (((1,), (1,)), ((), ())), preferred_element_type=F32)

    total = lax.fori_loop(0, BLK // 32, add, jnp.zeros((BLK, 2 * BLK), F32))
    cross = total[:, BLK:]
    total = total[:, :BLK] + cross + cross.T
    i = lax.broadcasted_iota(jnp.int32, (BLK, BLK), 0)
    j = lax.broadcasted_iota(jnp.int32, (BLK, BLK), 1)
    total = jnp.where(i % 8 == j % 8, total, 0.0)

    pick_rows = (lax.broadcasted_iota(jnp.int32, (REP, BLK), 0)
                 == replicas_of(place, lax.broadcasted_iota(jnp.int32, (REP, BLK), 1) // 8)).astype(F32)
    pick_cols = (lax.broadcasted_iota(jnp.int32, (BLK, 128), 1) % REP
                 == replicas_of(place, lax.broadcasted_iota(jnp.int32, (BLK, 128), 0) // 8)).astype(F32)
    gram = jnp.dot(jnp.dot(pick_rows, total, preferred_element_type=F32, precision=HIGH), pick_cols,
                   preferred_element_type=F32, precision=HIGH)
    lane = lax.broadcasted_iota(jnp.int32, (8, 128), 1)
    packed = jnp.zeros((8, 128), F32)
    for q in range(REP // 8):
        packed = packed + jnp.where(lane // REP == q, gram[8 * q:8 * q + 8], 0.0)
    sums_ref[0:8] = packed
    sums_ref[8:16] = jnp.where(lane % REP == replica_of(place, 0, 0), mean_ref[...], 0.0)
    for out in outs:
        out.wait()


def grads_and_sums(place, x_pieces, pieces, mean):
    layout = [(offset, piece.shape[-2], chunks) for piece, offset, chunks in pieces]
    any_spec = pl.BlockSpec(memory_space=pl.ANY)
    return pl.pallas_call(
        functools.partial(grads_kernel, layout),
        out_shape=(jax.ShapeDtypeStruct((REP, BLK, BLK), F32), jax.ShapeDtypeStruct((16, 128), F32)),
        in_specs=[pl.BlockSpec(memory_space=pltpu.SMEM)] + [any_spec] * (len(x_pieces) + len(layout))
        + [pl.BlockSpec(memory_space=pltpu.VMEM)],
        out_specs=(any_spec, pl.BlockSpec(memory_space=pltpu.VMEM)),
        scratch_shapes=[
            pltpu.VMEM((NY, NC, REP, TOK // (NY * NC), BLK), BF16),
            pltpu.VMEM((NX, NZ, TOK, BLK), BF16),
            pltpu.VMEM((REP, BLK, BLK), F32),
            pltpu.SemaphoreType.DMA((NY * NC,)),
            pltpu.SemaphoreType.DMA((len(layout), 2)),
            pltpu.SemaphoreType.DMA((NX,)),
        ],
        compiler_params=pltpu.CompilerParams(vmem_limit_bytes=58 * 2**20),
        cost_estimate=pl.CostEstimate(flops=6 * 10**9, bytes_accessed=24 * 2**20, transcendentals=0),
    )(place, *x_pieces, *[piece for piece, _, _ in pieces], mean)


def tree_weights(sums):
    lane = lax.broadcasted_iota(jnp.int32, (REP, 128), 1) % REP
    row = lax.broadcasted_iota(jnp.int32, (REP, 128), 0)
    inverse_lanes = float(NY * NC) / sums[8:9]
    inverse_rows = jnp.sum(jnp.where((lax.broadcasted_iota(jnp.int32, (REP, 128), 1) == row),
                                     jnp.broadcast_to(inverse_lanes, (REP, 128)), 0.0), axis=1, keepdims=True)
    wide = lax.broadcasted_iota(jnp.int32, (8, 128), 1)
    table = jnp.concatenate(
        [jnp.where(wide < REP, sums[0:8] if q == 0 else pltpu.roll(sums[0:8], 128 - REP * q, 1), 0.0)
         for q in range(REP // 8)], axis=0)
    table = table + pltpu.roll(table, REP, 1)
    table = table + pltpu.roll(table, 2 * REP, 1)
    table = table * inverse_rows * inverse_lanes
    factor = inverse_rows
    first = lax.broadcasted_iota(jnp.int32, (REP, 128), 1) < REP
    size = REP
    while size > 1:
        half = size // 2
        own = lane == row
        other_rows = lane == (row + half) % REP
        other_lanes = row == (lane + half) % REP
        own_r = jnp.sum(jnp.where(own & first, table, 0.0), axis=1, keepdims=True)
        cross_r = jnp.sum(jnp.where(other_rows & first, table, 0.0), axis=1, keepdims=True)
        own_l = jnp.sum(jnp.where(own, table, 0.0), axis=0, keepdims=True)
        cross_l = jnp.sum(jnp.where(other_lanes, table, 0.0), axis=0, keepdims=True)
        coef_r = 1.0 - cross_r / (2.0 * own_r + EPS_ADA)
        coef_l = 1.0 - cross_l / (2.0 * own_l + EPS_ADA)
        factor = factor * coef_r
        table = table * coef_r * coef_l
        table = table + pltpu.roll(table, half, 0)
        table = table + pltpu.roll(table, half, 1)
        size = half
    return jnp.broadcast_to(factor, (REP, 128))


def update_kernel(place, sums_ref, g_hbm, master_ref, one_ref, two_ref, weights_ref, master_out, one_out, two_out,
                  gv, factors, sem):
    copies = [pltpu.make_async_copy(g_hbm.at[r], gv.at[r], sem.at[r]) for r in range(REP)]
    for copy in copies:
        copy.start()
    factors[...] = tree_weights(sums_ref[...])
    for copy in copies:
        copy.wait()

    scales = [factors[pl.ds(replica_of(place, r // NZ, r % NZ), 1), :] for r in range(REP)]

    def strip(s, _):
        at = pl.ds(pl.multiple_of(s * 16, 16), 16)
        combined = jnp.zeros((16, BLK), F32)
        for r in range(REP):
            scale = scales[r]
            combined = combined + jnp.concatenate([scale, scale], axis=1) * gv[r, at, :]
        new_one = 0.9 * one_ref[at, :] + 0.1 * combined
        new_two = 0.95 * two_ref[at, :] + 0.05 * combined * combined
        first_hat = new_one / (1.0 - 0.9**STEP)
        second_hat = new_two / (1.0 - 0.95**STEP)
        master = master_ref[at, :]
        updated = master - 0.001 * (first_hat / (jnp.sqrt(second_hat) + 1e-08) + 0.1 * master)
        weights_ref[at, :] = updated.astype(BF16)
        master_out[at, :] = updated
        one_out[at, :] = new_one
        two_out[at, :] = new_two
        return 0

    lax.fori_loop(0, BLK // 16, strip, 0)


def update(place, sums, grads, master, one, two):
    vmem = pl.BlockSpec(memory_space=pltpu.VMEM)
    state = jax.ShapeDtypeStruct((BLK, BLK), F32)
    return pl.pallas_call(
        update_kernel,
        out_shape=(jax.ShapeDtypeStruct((BLK, BLK), BF16), state, state, state),
        in_specs=[pl.BlockSpec(memory_space=pltpu.SMEM), vmem, pl.BlockSpec(memory_space=pl.ANY), vmem, vmem, vmem],
        out_specs=(vmem,) * 4,
        scratch_shapes=[
            pltpu.VMEM((REP, BLK, BLK), F32),
            pltpu.VMEM((REP, 128), F32),
            pltpu.SemaphoreType.DMA((REP,)),
        ],
        compiler_params=pltpu.CompilerParams(vmem_limit_bytes=58 * 2**20),
        cost_estimate=pl.CostEstimate(flops=5 * 10**6, bytes_accessed=10 * 2**20, transcendentals=0),
    )(place, sums, grads, master, one, two)


def place_kernel(layout, place, *refs):
    count = len(layout)
    pieces, out_hbm, held, sem, out_sem = refs[:count], *refs[count:]
    copies = []
    for no, (offset, rows, chunks) in enumerate(layout):
        for index, kx, nx, kz, nz in chunks:
            source = pieces[no].at[index] if index else pieces[no]
            for i in range(nx * nz):
                r = replica_of(place, kx + i // nz, kz + i % nz)
                copies.append(pltpu.make_async_copy(
                    source.at[i], held.at[r, pl.ds(offset, rows)], sem.at[len(copies)]))
    for copy in copies:
        copy.start()
    for copy in copies:
        copy.wait()
    outs = []
    for part in range(8):
        at = pl.ds(part * REP // 8, REP // 8)
        outs.append(pltpu.make_async_copy(held.at[at], out_hbm.at[at], out_sem.at[part]))
        outs[-1].start()
    for out in outs:
        out.wait()


def place_rows(place, pieces):
    layout = [(offset, piece.shape[-2], chunks) for piece, offset, chunks in pieces]
    any_spec = pl.BlockSpec(memory_space=pl.ANY)
    total = 2 * REP
    return pl.pallas_call(
        functools.partial(place_kernel, layout),
        out_shape=jax.ShapeDtypeStruct((REP, BLK, BLK), BF16),
        in_specs=[pl.BlockSpec(memory_space=pltpu.SMEM)] + [any_spec] * len(layout),
        out_specs=any_spec,
        scratch_shapes=[
            pltpu.VMEM((REP, BLK, BLK), BF16),
            pltpu.SemaphoreType.DMA((total,)),
            pltpu.SemaphoreType.DMA((8,)),
        ],
        compiler_params=pltpu.CompilerParams(vmem_limit_bytes=56 * 2**20),
        cost_estimate=pl.CostEstimate(flops=0, bytes_accessed=8 * 2**20, transcendentals=0),
    )(place, *[piece for piece, _, _ in pieces])


def total_over_slice(sums):
    for axes, size in ((("x", "y"), NX * NY), (("z", "c"), NZ * NC)):
        sums = jnp.sum(lax.all_to_all(jnp.broadcast_to(sums[None], (size,) + sums.shape), axes, 0, 0), axis=0)
    return sums


def send_blocks(blocks, axis, size, at, core):
    turn = side(at, core)
    found = []
    for step in STEPS[:size]:
        sign = 1 if step % 2 else -1
        block = lax.dynamic_index_in_dim(blocks, lax.rem(at + sign * step * turn + size, size), 0, keepdims=False)
        if step:
            pairs = [(a * NC + c, (a + sign * step * side(a, c)) % size * NC + c)
                     for a in range(size) for c in range(NC)]
            block = lax.ppermute(block, (axis, "c"), pairs)
        found.append(block)
    return found


def exchange(token_rows, x, z, core):
    count = token_rows.shape[0]
    blocks = token_rows.reshape(count, NX, NZ, BLK).transpose(2, 1, 0, 3)
    line = jnp.stack(send_blocks(blocks, "z", NZ, z, core), axis=1)
    return jnp.concatenate(send_blocks(line, "x", NX, x, core))


def gather_tokens(own):
    ahead, behind = near(own, "y", NY, 1), near(own, "y", NY, -1)
    mine = [own, ahead, behind, near(ahead, "y", NY, -1)]
    return mine + [shift(piece, "c", NC, 1) for piece in mine]


def local(token_rows, advantage, cotangent, master, moment_one, moment_two):
    x, z, y, core = (lax.axis_index(name) for name in ("x", "z", "y", "c"))
    place = jnp.stack([x, z, side(x, core), side(z, core), y, core, side(y, core)]).astype(jnp.int32)
    x_pieces = gather_tokens(exchange(token_rows, x, z, core))
    weights = lax.all_gather(advantage, ("y", "c"), axis=0, tiled=True).astype(F32) * SCALE_FIXED
    weighted = (weights[:, None] * cotangent.astype(F32)).astype(BF16)
    mean = jnp.full((8, 128), jnp.sum(weights) / TOK)
    grads, sums = grads_and_sums(place, x_pieces, gather_plane(weighted, ROWS_A), mean)
    sums = total_over_slice(sums)
    new_weights, new_master, new_one, new_two = update(place, sums, grads, master, moment_one, moment_two)
    out = place_rows(place, gather_plane(new_weights, 128))
    return (out.reshape(REP * BLK, BLK), new_master, new_one, new_two)


def solution(mesh):
    fine = Mesh(mesh.devices.reshape(NX, NZ, NY, NC), ("x", "z", "y", "c"))
    dp, tensor = ("x", "z"), ("y", "c")
    state = P(dp, tensor)
    return jax.shard_map(
        local,
        mesh=fine,
        in_specs=(P(dp + tensor, None), P(dp + tensor), state, state, state, state),
        out_specs=(P(None, tensor), state, state, state),
        check_vma=False,
    )
```

```python
import functools
import jax
import jax.numpy as jnp
from jax import lax
from jax.experimental import pallas as pl
from jax.experimental.pallas import tpu as pltpu
from jax.sharding import Mesh, PartitionSpec as P

STEP = 10
SCALE_FIXED = 2.0 ** (-12)
EPS_ADA = 1e-06

NX, NZ, NY, NC = 4, 8, 4, 2
REP = NX * NZ
TOK = 512
BLK = 256
F32 = jnp.float32
BF16 = jnp.bfloat16
HIGH = lax.Precision.HIGHEST


def shift(array, axis, size, by):
    return lax.ppermute(array, axis, [(i, (i + by) % size) for i in range(size)])


def side(at, core):
    return 1 - 2 * ((at + core) % 2)


def near(array, axis, size, which):
    pairs = [(a * NC + c, (a + which * side(a, c)) % size * NC + c) for a in range(size) for c in range(NC)]
    return lax.ppermute(array, (axis, "c"), pairs)


def swapped_ring(block, axis, size):
    pair = jnp.stack([block, near(block, axis, size, 1)])
    found, held, which = [pair], pair, -1
    for _ in range(size // 2 - 1):
        held = near(held, axis, size, which)
        found.append(held)
        which = -which
    return found


def gather_plane(block):
    out = []
    for line in swapped_ring(block, "z", NZ):
        ahead, behind = near(line, "x", NX, 1), near(line, "x", NX, -1)
        out += [line, ahead, behind, near(ahead, "x", NX, -1)]
    return out


STEPS = (0, 1, -1, -2, 2, 3, -3, -4)


def step_of(k):
    return sum(jnp.where(k == i, step, 0) for i, step in enumerate(STEPS))


def replicas_of(place, slots):
    x = lax.rem(place[0] + place[2] * step_of(slots % NX) + NX, NX)
    z = lax.rem(place[1] + place[3] * step_of(slots // NX) + NZ, NZ)
    return x * NZ + z


def replica_of(place, slot):
    x = lax.rem(place[0] + place[2] * STEPS[slot % NX] + NX, NX)
    z = lax.rem(place[1] + place[3] * STEPS[slot // NX] + NZ, NZ)
    return x * NZ + z


def grads_kernel(count, place, *refs):
    tokens = NY * NC
    x_pieces, refs = refs[:tokens], refs[tokens:]
    pieces, (weights_ref, g_hbm, sums_ref) = refs[:count], refs[count:count + 3]
    xv, wv, gv, xsem, wsem, gsem = refs[count + 3:]
    y, core, turn = place[4], place[5], place[6]
    parts = []
    for no in range(tokens):
        c = core if no < NY else 1 - core
        row = lax.rem(y + (turn if no < NY else -turn) * STEPS[no % NY] + NY, NY)
        parts.append(pltpu.make_async_copy(x_pieces[no], xv.at[row, c], xsem.at[no]))
    loads = [pltpu.make_async_copy(pieces[no], wv.at[pl.ds(no // NX * 2, 2), no % NX], wsem.at[no])
             for no in range(count)]
    for copy in parts + loads:
        copy.start()
    for copy in parts:
        copy.wait()

    def multiply(slot, _):
        rows = xv[:, :, replicas_of(place, slot)].reshape(TOK, BLK)
        gv[slot] = lax.dot_general(rows, wv[slot // NX, lax.rem(slot, NX)], (((0,), (0,)), ((), ())),
                                   preferred_element_type=F32)
        return 0

    outs = []
    for part in range(count // NX):
        for copy in loads[part * NX:(part + 1) * NX]:
            copy.wait()
        lax.fori_loop(part * 2 * NX, (part + 1) * 2 * NX, multiply, 0, unroll=2)
        at = pl.ds(part * 2 * NX, 2 * NX)
        outs.append(pltpu.make_async_copy(gv.at[at], g_hbm.at[at], gsem.at[part]))
        outs[-1].start()

    def add(j, total):
        y = jnp.concatenate(
            [gv[:, pl.ds(pl.multiple_of(j * 32 + 8 * h, 8), 8), :].reshape(BLK, BLK) for h in range(4)], axis=1)
        high = y.astype(BF16)
        low = (y - high.astype(F32)).astype(BF16)
        both = jnp.concatenate([high, low], axis=0)
        return total + lax.dot_general(high, both, (((1,), (1,)), ((), ())), preferred_element_type=F32)

    total = lax.fori_loop(0, BLK // 32, add, jnp.zeros((BLK, 2 * BLK), F32))
    cross = total[:, BLK:]
    total = total[:, :BLK] + cross + cross.T
    i = lax.broadcasted_iota(jnp.int32, (BLK, BLK), 0)
    j = lax.broadcasted_iota(jnp.int32, (BLK, BLK), 1)
    total = jnp.where(i % 8 == j % 8, total, 0.0)

    pick_rows = (lax.broadcasted_iota(jnp.int32, (REP, BLK), 0)
                 == replicas_of(place, lax.broadcasted_iota(jnp.int32, (REP, BLK), 1) // 8)).astype(F32)
    pick_cols = (lax.broadcasted_iota(jnp.int32, (BLK, 128), 1) % REP
                 == replicas_of(place, lax.broadcasted_iota(jnp.int32, (BLK, 128), 0) // 8)).astype(F32)
    gram = jnp.dot(jnp.dot(pick_rows, total, preferred_element_type=F32, precision=HIGH), pick_cols,
                   preferred_element_type=F32, precision=HIGH)
    lane = lax.broadcasted_iota(jnp.int32, (8, 128), 1)
    packed = jnp.zeros((8, 128), F32)
    for q in range(REP // 8):
        packed = packed + jnp.where(lane // REP == q, gram[8 * q:8 * q + 8], 0.0)
    mean = jnp.sum(weights_ref[...], axis=(0, 1), keepdims=True) / TOK
    means = jnp.where(lane % REP == place[0] * NZ + place[1], mean, 0.0)
    for copy in range(sums_ref.shape[0]):
        sums_ref[copy, 0:8] = packed
        sums_ref[copy, 8:16] = means
    for out in outs:
        out.wait()


def grads_and_sums(place, x_pieces, pieces, weights):
    any_spec = pl.BlockSpec(memory_space=pl.ANY)
    return pl.pallas_call(
        functools.partial(grads_kernel, len(pieces)),
        out_shape=(jax.ShapeDtypeStruct((REP, BLK, BLK), F32), jax.ShapeDtypeStruct((NX * NY, 16, 128), F32)),
        in_specs=[pl.BlockSpec(memory_space=pltpu.SMEM)] + [any_spec] * (len(x_pieces) + len(pieces))
        + [pl.BlockSpec(memory_space=pltpu.VMEM)],
        out_specs=(any_spec, pl.BlockSpec(memory_space=pltpu.VMEM)),
        scratch_shapes=[
            pltpu.VMEM((NY, NC, REP, TOK // (NY * NC), BLK), BF16),
            pltpu.VMEM((NZ, NX, TOK, BLK), BF16),
            pltpu.VMEM((REP, BLK, BLK), F32),
            pltpu.SemaphoreType.DMA((NY * NC,)),
            pltpu.SemaphoreType.DMA((len(pieces),)),
            pltpu.SemaphoreType.DMA((NX,)),
        ],
        compiler_params=pltpu.CompilerParams(vmem_limit_bytes=58 * 2**20),
        cost_estimate=pl.CostEstimate(flops=6 * 10**9, bytes_accessed=24 * 2**20, transcendentals=0),
    )(place, *x_pieces, *pieces, weights)


def tree_weights(sums):
    lane = lax.broadcasted_iota(jnp.int32, (REP, 128), 1) % REP
    row = lax.broadcasted_iota(jnp.int32, (REP, 128), 0)
    inverse_lanes = float(NY * NC) / sums[8:9]
    inverse_rows = jnp.sum(jnp.where((lax.broadcasted_iota(jnp.int32, (REP, 128), 1) == row),
                                     jnp.broadcast_to(inverse_lanes, (REP, 128)), 0.0), axis=1, keepdims=True)
    wide = lax.broadcasted_iota(jnp.int32, (8, 128), 1)
    table = jnp.concatenate(
        [jnp.where(wide < REP, sums[0:8] if q == 0 else pltpu.roll(sums[0:8], 128 - REP * q, 1), 0.0)
         for q in range(REP // 8)], axis=0)
    table = table + pltpu.roll(table, REP, 1)
    table = table + pltpu.roll(table, 2 * REP, 1)
    table = table * inverse_rows * inverse_lanes
    factor = inverse_rows
    first = lax.broadcasted_iota(jnp.int32, (REP, 128), 1) < REP
    size = REP
    while size > 1:
        half = size // 2
        own = lane == row
        other_rows = lane == (row + half) % REP
        other_lanes = row == (lane + half) % REP
        own_r = jnp.sum(jnp.where(own & first, table, 0.0), axis=1, keepdims=True)
        cross_r = jnp.sum(jnp.where(other_rows & first, table, 0.0), axis=1, keepdims=True)
        own_l = jnp.sum(jnp.where(own, table, 0.0), axis=0, keepdims=True)
        cross_l = jnp.sum(jnp.where(other_lanes, table, 0.0), axis=0, keepdims=True)
        coef_r = 1.0 - cross_r / (2.0 * own_r + EPS_ADA)
        coef_l = 1.0 - cross_l / (2.0 * own_l + EPS_ADA)
        factor = factor * coef_r
        table = table * coef_r * coef_l
        table = table + pltpu.roll(table, half, 0)
        table = table + pltpu.roll(table, half, 1)
        size = half
    return jnp.broadcast_to(factor, (REP, 128))


def update_kernel(place, sums_ref, g_hbm, master_ref, one_ref, two_ref, weights_ref, master_out, one_out, two_out,
                  gv, total, factors, sem):
    group = 4
    copies = [pltpu.make_async_copy(g_hbm.at[pl.ds(r, group)], gv.at[pl.ds(r, group)], sem.at[r])
              for r in range(0, REP, group)]
    for copy in copies:
        copy.start()
    factors[...] = tree_weights(jnp.sum(sums_ref[...], axis=0))

    for no, copy in enumerate(copies):
        scales = []
        for r in range(no * group, (no + 1) * group):
            scale = factors[pl.ds(replica_of(place, r), 1), :]
            scales.append(jnp.concatenate([scale, scale], axis=1))
        copy.wait()

        def strip(s, _):
            at = pl.ds(pl.multiple_of(s * 32, 32), 32)
            part = scales[0] * gv[no * group, at, :]
            for r in range(1, group):
                part = part + scales[r] * gv[no * group + r, at, :]
            total[at, :] = total[at, :] + part if no else part
            return 0

        lax.fori_loop(0, BLK // 32, strip, 0, unroll=2)

    combined = total[...]
    new_one = 0.9 * one_ref[...] + 0.1 * combined
    new_two = 0.95 * two_ref[...] + 0.05 * combined * combined
    first_hat = new_one / (1.0 - 0.9**STEP)
    second_hat = new_two / (1.0 - 0.95**STEP)
    master = master_ref[...]
    updated = master - 0.001 * (first_hat / (jnp.sqrt(second_hat) + 1e-08) + 0.1 * master)
    weights_ref[...] = updated.astype(BF16)
    master_out[...] = updated
    one_out[...] = new_one
    two_out[...] = new_two


def update(place, sums, grads, master, one, two):
    vmem = pl.BlockSpec(memory_space=pltpu.VMEM)
    state = jax.ShapeDtypeStruct((BLK, BLK), F32)
    return pl.pallas_call(
        update_kernel,
        out_shape=(jax.ShapeDtypeStruct((BLK, BLK), BF16), state, state, state),
        in_specs=[pl.BlockSpec(memory_space=pltpu.SMEM), vmem, pl.BlockSpec(memory_space=pl.ANY), vmem, vmem, vmem],
        out_specs=(vmem,) * 4,
        scratch_shapes=[
            pltpu.VMEM((REP, BLK, BLK), F32),
            pltpu.VMEM((BLK, BLK), F32),
            pltpu.VMEM((REP, 128), F32),
            pltpu.SemaphoreType.DMA((REP,)),
        ],
        compiler_params=pltpu.CompilerParams(vmem_limit_bytes=58 * 2**20),
        cost_estimate=pl.CostEstimate(flops=5 * 10**6, bytes_accessed=10 * 2**20, transcendentals=0),
    )(place, sums, grads, master, one, two)


def place_kernel(first, count, place, *refs):
    pieces, out_hbm, held, sem, out_sem = refs[:count], *refs[-4:]
    copies, outs = [], []
    for no in range(count):
        for i in range(2):
            slot = ((first + no) // NX * 2 + i) * NX + no % NX
            at = no * 2 + i
            copies.append(pltpu.make_async_copy(pieces[no].at[i], held.at[at], sem.at[at]))
            outs.append(pltpu.make_async_copy(held.at[at], out_hbm.at[replica_of(place, slot)], out_sem.at[at]))
    for copy in copies:
        copy.start()
    for copy, out in zip(copies, outs):
        copy.wait()
        out.start()
    for out in outs:
        out.wait()


def place_rows(place, pieces, first, out):
    any_spec = pl.BlockSpec(memory_space=pl.ANY)
    count = len(pieces)
    return pl.pallas_call(
        functools.partial(place_kernel, first, count),
        out_shape=jax.ShapeDtypeStruct((REP, BLK, BLK), BF16),
        in_specs=[pl.BlockSpec(memory_space=pltpu.SMEM)] + [any_spec] * (count + len(out)),
        out_specs=any_spec,
        scratch_shapes=[
            pltpu.VMEM((2 * count, BLK, BLK), BF16),
            pltpu.SemaphoreType.DMA((2 * count,)),
            pltpu.SemaphoreType.DMA((2 * count,)),
        ],
        input_output_aliases={1 + count: 0} if out else {},
        compiler_params=pltpu.CompilerParams(vmem_limit_bytes=56 * 2**20),
        cost_estimate=pl.CostEstimate(flops=0, bytes_accessed=2**18 * count, transcendentals=0),
    )(place, *pieces, *out)


def totals_of_groups(sums):
    sums = jnp.sum(lax.all_to_all(sums, ("x", "y"), 0, 0), axis=0)
    return lax.all_to_all(jnp.broadcast_to(sums[None], (NZ * NC,) + sums.shape), ("z", "c"), 0, 0)


def gather_tokens(own):
    ahead, behind = near(own, "y", NY, 1), near(own, "y", NY, -1)
    mine = [own, ahead, behind, near(ahead, "y", NY, -1)]
    return mine + [shift(piece, "c", NC, 1) for piece in mine]


def local(token_rows, advantage, cotangent, master, moment_one, moment_two):
    x, z, y, core = (lax.axis_index(name) for name in ("x", "z", "y", "c"))
    place = jnp.stack([x, z, side(x, core), side(z, core), y, core, side(y, core)]).astype(jnp.int32)
    weights = lax.all_gather(advantage, ("y", "c"), axis=0, tiled=True).astype(F32) * SCALE_FIXED
    weighted = (weights[:, None] * cotangent.astype(F32)).astype(BF16)
    own = lax.all_to_all(token_rows, ("x", "z"), 1, 0, tiled=True).reshape(REP, -1, BLK)
    x_pieces = gather_tokens(own)
    grads, sums = grads_and_sums(place, x_pieces, gather_plane(weighted), weights.reshape(-1, 128))
    sums = totals_of_groups(sums)
    new_weights, new_master, new_one, new_two = update(place, sums, grads, master, moment_one, moment_two)
    pieces = gather_plane(new_weights)
    early = len(pieces) - NX
    out = place_rows(place, pieces[:early], 0, ())
    out = place_rows(place, pieces[early:], early, (out,))
    return (out.reshape(REP * BLK, BLK), new_master, new_one, new_two)


def solution(mesh):
    fine = Mesh(mesh.devices.reshape(NX, NZ, NY, NC), ("x", "z", "y", "c"))
    dp, tensor = ("x", "z"), ("y", "c")
    state = P(dp, tensor)
    return jax.shard_map(
        local,
        mesh=fine,
        in_specs=(P(dp + tensor, None), P(dp + tensor), state, state, state, state),
        out_specs=(P(None, tensor), state, state, state),
        check_vma=False,
    )
```

```python
import functools
import jax
import jax.numpy as jnp
from jax import lax
from jax.experimental import pallas as pl
from jax.experimental.pallas import tpu as pltpu
from jax.sharding import Mesh, PartitionSpec as P

STEP = 10
SCALE_FIXED = 2.0 ** (-12)
EPS_ADA = 1e-06

NX, NZ, NY, NC = 4, 8, 4, 2
REP = NX * NZ
TOK = 512
BLK = 256
ROWS_A = 352
CHUNKS = 2
F32 = jnp.float32
BF16 = jnp.bfloat16
HIGH = lax.Precision.HIGHEST


def shift(array, axis, size, by):
    return lax.ppermute(array, axis, [(i, (i + by) % size) for i in range(size)])


def side(at, core):
    return 1 - 2 * ((at + core) % 2)


def near(array, axis, size, which):
    pairs = [(a * NC + c, (a + which * side(a, c)) % size * NC + c) for a in range(size) for c in range(NC)]
    return lax.ppermute(array, (axis, "c"), pairs)


def swapped_ring(block, axis, size):
    held, which = jnp.stack([block, near(block, axis, size, 1)]), -1
    found = [held]
    for _ in range(size // 2 - 1):
        held = near(held, axis, size, which)
        found.append(held)
        which = -which
    return found


def gather_plane(block, cut, chunks):
    out, kz = [], 0
    lines = swapped_ring(block[:cut], "z", NZ)
    for chunk in range(chunks):
        line = lines[chunk * 4 // chunks:(chunk + 1) * 4 // chunks]
        line = line[0] if len(line) == 1 else jnp.concatenate(line)
        ahead, behind = near(line, "x", NX, 1), near(line, "x", NX, -1)
        for kx, piece in enumerate((line, ahead, behind, near(ahead, "x", NX, -1))):
            out.append((piece[:, None], 0, kz, kx))
        kz += line.shape[0]
    if cut < block.shape[0]:
        for no, piece in enumerate(swapped_ring(jnp.concatenate(swapped_ring(block[cut:], "x", NX)), "z", NZ)):
            out.append((piece, cut, 2 * no, 0))
    return out


STEPS = (0, 1, -1, -2, 2, 3, -3, -4)


def step_of(k):
    return sum(jnp.where(k == i, step, 0) for i, step in enumerate(STEPS))


def replicas_of(place, slots):
    x = lax.rem(place[0] + place[2] * step_of(slots % NX) + NX, NX)
    z = lax.rem(place[1] + place[3] * step_of(slots // NX) + NZ, NZ)
    return x * NZ + z


def replica_of(place, slot):
    x = lax.rem(place[0] + place[2] * STEPS[slot % NX] + NX, NX)
    z = lax.rem(place[1] + place[3] * STEPS[slot // NX] + NZ, NZ)
    return x * NZ + z


def grads_kernel(layout, place, *refs):
    tokens = NY * NC
    x_pieces, refs = refs[:tokens], refs[tokens:]
    count = len(layout)
    pieces, (weights_ref, g_hbm, sums_ref) = refs[:count], refs[count:count + 3]
    xv, wv, gv, xsem, wsem, gsem = refs[count + 3:]
    y, core, turn = place[4], place[5], place[6]
    parts = []
    for no in range(tokens):
        c = core if no < NY else 1 - core
        row = lax.rem(y + (turn if no < NY else -turn) * STEPS[no % NY] + NY, NY)
        parts.append(pltpu.make_async_copy(x_pieces[no], xv.at[row, c], xsem.at[no]))
    loads = []
    for no, ((nz, nx, rows, _), offset, kz, kx) in enumerate(layout):
        loads.append(pltpu.make_async_copy(
            pieces[no], wv.at[pl.ds(kz, nz), pl.ds(kx, nx), pl.ds(offset, rows)], wsem.at[no]))
    for copy in parts + loads:
        copy.start()
    for copy in parts:
        copy.wait()

    def multiply(slot, _):
        rows = xv[:, :, replicas_of(place, slot)].reshape(TOK, BLK)
        gv[slot] = lax.dot_general(rows, wv[slot // NX, lax.rem(slot, NX)], (((0,), (0,)), ((), ())),
                                   preferred_element_type=F32)
        return 0

    outs = []
    waited = set()
    for part in range(NZ // 2):
        for no, (_, _, kz, _) in enumerate(layout):
            if kz < 2 * part + 2 and no not in waited:
                loads[no].wait()
                waited.add(no)
        lax.fori_loop(part * 2 * NX, (part + 1) * 2 * NX, multiply, 0, unroll=2)
        at = pl.ds(part * 2 * NX, 2 * NX)
        outs.append(pltpu.make_async_copy(gv.at[at], g_hbm.at[at], gsem.at[part]))
        outs[-1].start()

    def add(j, total):
        y = jnp.concatenate(
            [gv[:, pl.ds(pl.multiple_of(j * 32 + 8 * h, 8), 8), :].reshape(BLK, BLK) for h in range(4)], axis=1)
        high = y.astype(BF16)
        low = (y - high.astype(F32)).astype(BF16)
        both = jnp.concatenate([high, low], axis=0)
        return total + lax.dot_general(high, both, (((1,), (1,)), ((), ())), preferred_element_type=F32)

    total = lax.fori_loop(0, BLK // 32, add, jnp.zeros((BLK, 2 * BLK), F32))
    cross = total[:, BLK:]
    total = total[:, :BLK] + cross + cross.T
    i = lax.broadcasted_iota(jnp.int32, (BLK, BLK), 0)
    j = lax.broadcasted_iota(jnp.int32, (BLK, BLK), 1)
    total = jnp.where(i % 8 == j % 8, total, 0.0)

    pick_rows = (lax.broadcasted_iota(jnp.int32, (REP, BLK), 0)
                 == replicas_of(place, lax.broadcasted_iota(jnp.int32, (REP, BLK), 1) // 8)).astype(F32)
    pick_cols = (lax.broadcasted_iota(jnp.int32, (BLK, 128), 1) % REP
                 == replicas_of(place, lax.broadcasted_iota(jnp.int32, (BLK, 128), 0) // 8)).astype(F32)
    gram = jnp.dot(jnp.dot(pick_rows, total, preferred_element_type=F32, precision=HIGH), pick_cols,
                   preferred_element_type=F32, precision=HIGH)
    lane = lax.broadcasted_iota(jnp.int32, (8, 128), 1)
    packed = jnp.zeros((8, 128), F32)
    for q in range(REP // 8):
        packed = packed + jnp.where(lane // REP == q, gram[8 * q:8 * q + 8], 0.0)
    mean = jnp.sum(weights_ref[...], axis=(0, 1), keepdims=True) / TOK
    means = jnp.where(lane % REP == place[0] * NZ + place[1], mean, 0.0)
    for copy in range(sums_ref.shape[0]):
        sums_ref[copy, 0:8] = packed
        sums_ref[copy, 8:16] = means
    for out in outs:
        out.wait()


def grads_and_sums(place, x_pieces, pieces, weights):
    layout = [(piece.shape, *where) for piece, *where in pieces]
    any_spec = pl.BlockSpec(memory_space=pl.ANY)
    return pl.pallas_call(
        functools.partial(grads_kernel, layout),
        out_shape=(jax.ShapeDtypeStruct((REP, BLK, BLK), F32), jax.ShapeDtypeStruct((NX * NY, 16, 128), F32)),
        in_specs=[pl.BlockSpec(memory_space=pltpu.SMEM)] + [any_spec] * (len(x_pieces) + len(pieces))
        + [pl.BlockSpec(memory_space=pltpu.VMEM)],
        out_specs=(any_spec, pl.BlockSpec(memory_space=pltpu.VMEM)),
        scratch_shapes=[
            pltpu.VMEM((NY, NC, REP, TOK // (NY * NC), BLK), BF16),
            pltpu.VMEM((NZ, NX, TOK, BLK), BF16),
            pltpu.VMEM((REP, BLK, BLK), F32),
            pltpu.SemaphoreType.DMA((NY * NC,)),
            pltpu.SemaphoreType.DMA((len(pieces),)),
            pltpu.SemaphoreType.DMA((NX,)),
        ],
        compiler_params=pltpu.CompilerParams(vmem_limit_bytes=58 * 2**20),
        cost_estimate=pl.CostEstimate(flops=6 * 10**9, bytes_accessed=24 * 2**20, transcendentals=0),
    )(place, *x_pieces, *[piece for piece, *_ in pieces], weights)


def tree_weights(sums):
    lane = lax.broadcasted_iota(jnp.int32, (REP, 128), 1) % REP
    row = lax.broadcasted_iota(jnp.int32, (REP, 128), 0)
    inverse_lanes = float(NY * NC) / sums[8:9]
    inverse_rows = jnp.sum(jnp.where((lax.broadcasted_iota(jnp.int32, (REP, 128), 1) == row),
                                     jnp.broadcast_to(inverse_lanes, (REP, 128)), 0.0), axis=1, keepdims=True)
    wide = lax.broadcasted_iota(jnp.int32, (8, 128), 1)
    table = jnp.concatenate(
        [jnp.where(wide < REP, sums[0:8] if q == 0 else pltpu.roll(sums[0:8], 128 - REP * q, 1), 0.0)
         for q in range(REP // 8)], axis=0)
    table = table + pltpu.roll(table, REP, 1)
    table = table + pltpu.roll(table, 2 * REP, 1)
    table = table * inverse_rows * inverse_lanes
    factor = inverse_rows
    first = lax.broadcasted_iota(jnp.int32, (REP, 128), 1) < REP
    size = REP
    while size > 1:
        half = size // 2
        own = lane == row
        other_rows = lane == (row + half) % REP
        other_lanes = row == (lane + half) % REP
        own_r = jnp.sum(jnp.where(own & first, table, 0.0), axis=1, keepdims=True)
        cross_r = jnp.sum(jnp.where(other_rows & first, table, 0.0), axis=1, keepdims=True)
        own_l = jnp.sum(jnp.where(own, table, 0.0), axis=0, keepdims=True)
        cross_l = jnp.sum(jnp.where(other_lanes, table, 0.0), axis=0, keepdims=True)
        coef_r = 1.0 - cross_r / (2.0 * own_r + EPS_ADA)
        coef_l = 1.0 - cross_l / (2.0 * own_l + EPS_ADA)
        factor = factor * coef_r
        table = table * coef_r * coef_l
        table = table + pltpu.roll(table, half, 0)
        table = table + pltpu.roll(table, half, 1)
        size = half
    return jnp.broadcast_to(factor, (REP, 128))


def update_kernel(place, sums_ref, g_hbm, master_ref, one_ref, two_ref, weights_ref, master_out, one_out, two_out,
                  gv, total, factors, sem):
    group = 4
    copies = [pltpu.make_async_copy(g_hbm.at[pl.ds(r, group)], gv.at[pl.ds(r, group)], sem.at[r])
              for r in range(0, REP, group)]
    for copy in copies:
        copy.start()
    factors[...] = tree_weights(jnp.sum(sums_ref[...], axis=0))

    for no, copy in enumerate(copies):
        scales = []
        for r in range(no * group, (no + 1) * group):
            scale = factors[pl.ds(replica_of(place, r), 1), :]
            scales.append(jnp.concatenate([scale, scale], axis=1))
        copy.wait()

        def strip(s, _):
            at = pl.ds(pl.multiple_of(s * 32, 32), 32)
            part = scales[0] * gv[no * group, at, :]
            for r in range(1, group):
                part = part + scales[r] * gv[no * group + r, at, :]
            total[at, :] = total[at, :] + part if no else part
            return 0

        lax.fori_loop(0, BLK // 32, strip, 0, unroll=2)

    combined = total[...]
    new_one = 0.9 * one_ref[...] + 0.1 * combined
    new_two = 0.95 * two_ref[...] + 0.05 * combined * combined
    first_hat = new_one / (1.0 - 0.9**STEP)
    second_hat = new_two / (1.0 - 0.95**STEP)
    master = master_ref[...]
    updated = master - 0.001 * (first_hat / (jnp.sqrt(second_hat) + 1e-08) + 0.1 * master)
    weights_ref[...] = updated.astype(BF16)
    master_out[...] = updated
    one_out[...] = new_one
    two_out[...] = new_two


def update(place, sums, grads, master, one, two):
    vmem = pl.BlockSpec(memory_space=pltpu.VMEM)
    state = jax.ShapeDtypeStruct((BLK, BLK), F32)
    return pl.pallas_call(
        update_kernel,
        out_shape=(jax.ShapeDtypeStruct((BLK, BLK), BF16), state, state, state),
        in_specs=[pl.BlockSpec(memory_space=pltpu.SMEM), vmem, pl.BlockSpec(memory_space=pl.ANY), vmem, vmem, vmem],
        out_specs=(vmem,) * 4,
        scratch_shapes=[
            pltpu.VMEM((REP, BLK, BLK), F32),
            pltpu.VMEM((BLK, BLK), F32),
            pltpu.VMEM((REP, 128), F32),
            pltpu.SemaphoreType.DMA((REP,)),
        ],
        compiler_params=pltpu.CompilerParams(vmem_limit_bytes=58 * 2**20),
        cost_estimate=pl.CostEstimate(flops=5 * 10**6, bytes_accessed=10 * 2**20, transcendentals=0),
    )(place, sums, grads, master, one, two)


def place_kernel(first, count, place, *refs):
    pieces, out_hbm, held, sem, out_sem = refs[:count], *refs[-4:]
    copies, outs = [], []
    for no in range(count):
        for i in range(2):
            slot = ((first + no) // NX * 2 + i) * NX + no % NX
            at = no * 2 + i
            copies.append(pltpu.make_async_copy(pieces[no].at[i], held.at[at], sem.at[at]))
            outs.append(pltpu.make_async_copy(held.at[at], out_hbm.at[replica_of(place, slot)], out_sem.at[at]))
    for copy in copies:
        copy.start()
    for copy, out in zip(copies, outs):
        copy.wait()
        out.start()
    for out in outs:
        out.wait()


def place_rows(place, pieces, first, out):
    any_spec = pl.BlockSpec(memory_space=pl.ANY)
    count = len(pieces)
    return pl.pallas_call(
        functools.partial(place_kernel, first, count),
        out_shape=jax.ShapeDtypeStruct((REP, BLK, BLK), BF16),
        in_specs=[pl.BlockSpec(memory_space=pltpu.SMEM)] + [any_spec] * (count + len(out)),
        out_specs=any_spec,
        scratch_shapes=[
            pltpu.VMEM((2 * count, BLK, BLK), BF16),
            pltpu.SemaphoreType.DMA((2 * count,)),
            pltpu.SemaphoreType.DMA((2 * count,)),
        ],
        input_output_aliases={1 + count: 0} if out else {},
        compiler_params=pltpu.CompilerParams(vmem_limit_bytes=56 * 2**20),
        cost_estimate=pl.CostEstimate(flops=0, bytes_accessed=2**18 * count, transcendentals=0),
    )(place, *pieces, *out)


def totals_of_groups(sums):
    sums = jnp.sum(lax.all_to_all(sums, ("x", "y"), 0, 0), axis=0)
    return lax.all_to_all(jnp.broadcast_to(sums[None], (NZ * NC,) + sums.shape), ("z", "c"), 0, 0)


def gather_tokens(own):
    ahead, behind = near(own, "y", NY, 1), near(own, "y", NY, -1)
    mine = [own, ahead, behind, near(ahead, "y", NY, -1)]
    return mine + [shift(piece, "c", NC, 1) for piece in mine]


def local(token_rows, advantage, cotangent, master, moment_one, moment_two):
    x, z, y, core = (lax.axis_index(name) for name in ("x", "z", "y", "c"))
    place = jnp.stack([x, z, side(x, core), side(z, core), y, core, side(y, core)]).astype(jnp.int32)
    weights = lax.all_gather(advantage, ("y", "c"), axis=0, tiled=True).astype(F32) * SCALE_FIXED
    weighted = (weights[:, None] * cotangent.astype(F32)).astype(BF16)
    own = lax.all_to_all(token_rows, ("x", "z"), 1, 0, tiled=True).reshape(REP, -1, BLK)
    x_pieces = gather_tokens(own)
    grads, sums = grads_and_sums(place, x_pieces, gather_plane(weighted, ROWS_A, CHUNKS), weights.reshape(-1, 128))
    sums = totals_of_groups(sums)
    new_weights, new_master, new_one, new_two = update(place, sums, grads, master, moment_one, moment_two)
    pieces = [piece[:, 0] for piece, *_ in gather_plane(new_weights, BLK, 4)]
    early = len(pieces) - NX
    out = place_rows(place, pieces[:early], 0, ())
    out = place_rows(place, pieces[early:], early, (out,))
    return (out.reshape(REP * BLK, BLK), new_master, new_one, new_two)


def solution(mesh):
    fine = Mesh(mesh.devices.reshape(NX, NZ, NY, NC), ("x", "z", "y", "c"))
    dp, tensor = ("x", "z"), ("y", "c")
    state = P(dp, tensor)
    return jax.shard_map(
        local,
        mesh=fine,
        in_specs=(P(dp + tensor, None), P(dp + tensor), state, state, state, state),
        out_specs=(P(None, tensor), state, state, state),
        check_vma=False,
    )
```

```python
import functools
import jax
import jax.numpy as jnp
from jax import lax
from jax.experimental import pallas as pl
from jax.experimental.pallas import tpu as pltpu
from jax.sharding import Mesh, PartitionSpec as P

STEP = 10
SCALE_FIXED = 2.0 ** (-12)
EPS_ADA = 1e-06

NX, NZ, NY, NC = 4, 8, 4, 2
REP = NX * NZ
TOK = 512
BLK = 256
ROWS_A = 352
CHUNKS = 2
F32 = jnp.float32
BF16 = jnp.bfloat16
HIGH = lax.Precision.HIGHEST


def shift(array, axis, size, by):
    return lax.ppermute(array, axis, [(i, (i + by) % size) for i in range(size)])


def side(at, core):
    return 1 - 2 * ((at + core) % 2)


def near(array, axis, size, which):
    pairs = [(a * NC + c, (a + which * side(a, c)) % size * NC + c) for a in range(size) for c in range(NC)]
    return lax.ppermute(array, (axis, "c"), pairs)


def swapped_ring(block, axis, size):
    held, which = jnp.stack([block, near(block, axis, size, 1)]), -1
    found = [held]
    for _ in range(size // 2 - 1):
        held = near(held, axis, size, which)
        found.append(held)
        which = -which
    return found


def gather_plane(block, cut, chunks):
    out, kz = [], 0
    lines = swapped_ring(block[:cut], "z", NZ)
    for chunk in range(chunks):
        line = lines[chunk * 4 // chunks:(chunk + 1) * 4 // chunks]
        line = line[0] if len(line) == 1 else jnp.concatenate(line)
        ahead, behind = near(line, "x", NX, 1), near(line, "x", NX, -1)
        for kx, piece in enumerate((line, ahead, behind, near(ahead, "x", NX, -1))):
            out.append((piece[:, None], 0, kz, kx))
        kz += line.shape[0]
    if cut < block.shape[0]:
        for no, piece in enumerate(swapped_ring(jnp.concatenate(swapped_ring(block[cut:], "x", NX)), "z", NZ)):
            out.append((piece, cut, 2 * no, 0))
    return out


STEPS = (0, 1, -1, -2, 2, 3, -3, -4)


def step_of(k):
    return sum(jnp.where(k == i, step, 0) for i, step in enumerate(STEPS))


def replicas_of(place, slots):
    x = lax.rem(place[0] + place[2] * step_of(slots % NX) + NX, NX)
    z = lax.rem(place[1] + place[3] * step_of(slots // NX) + NZ, NZ)
    return x * NZ + z


def replica_of(place, slot):
    x = lax.rem(place[0] + place[2] * STEPS[slot % NX] + NX, NX)
    z = lax.rem(place[1] + place[3] * STEPS[slot // NX] + NZ, NZ)
    return x * NZ + z


def grads_kernel(layout, place, *refs):
    tokens = NY * NC
    x_pieces, refs = refs[:tokens], refs[tokens:]
    count = len(layout)
    pieces, (weights_ref, g_hbm, sums_ref) = refs[:count], refs[count:count + 3]
    xv, wv, gv, xsem, wsem, gsem = refs[count + 3:]
    y, core, turn = place[4], place[5], place[6]
    parts = []
    for no in range(tokens):
        c = core if no < NY else 1 - core
        row = lax.rem(y + (turn if no < NY else -turn) * STEPS[no % NY] + NY, NY)
        parts.append(pltpu.make_async_copy(x_pieces[no], xv.at[row, c], xsem.at[no]))
    loads = []
    for no, ((nz, nx, rows, _), offset, kz, kx) in enumerate(layout):
        loads.append(pltpu.make_async_copy(
            pieces[no], wv.at[pl.ds(kz, nz), pl.ds(kx, nx), pl.ds(offset, rows)], wsem.at[no]))
    for copy in parts + loads:
        copy.start()
    for copy in parts:
        copy.wait()

    def multiply(slot, _):
        rows = xv[:, :, replicas_of(place, slot)].reshape(TOK, BLK)
        gv[slot] = lax.dot_general(rows, wv[slot // NX, lax.rem(slot, NX)], (((0,), (0,)), ((), ())),
                                   preferred_element_type=F32)
        return 0

    outs = []
    waited = set()
    for part in range(NZ // 2):
        for no, (_, _, kz, _) in enumerate(layout):
            if kz < 2 * part + 2 and no not in waited:
                loads[no].wait()
                waited.add(no)
        lax.fori_loop(part * 2 * NX, (part + 1) * 2 * NX, multiply, 0, unroll=8)
        at = pl.ds(part * 2 * NX, 2 * NX)
        outs.append(pltpu.make_async_copy(gv.at[at], g_hbm.at[at], gsem.at[part]))
        outs[-1].start()

    def add(j, total):
        y = jnp.concatenate(
            [gv[:, pl.ds(pl.multiple_of(j * 32 + 8 * h, 8), 8), :].reshape(BLK, BLK) for h in range(4)], axis=1)
        high = y.astype(BF16)
        low = (y - high.astype(F32)).astype(BF16)
        both = jnp.concatenate([high, low], axis=0)
        return total + lax.dot_general(high, both, (((1,), (1,)), ((), ())), preferred_element_type=F32)

    total = lax.fori_loop(0, BLK // 32, add, jnp.zeros((BLK, 2 * BLK), F32), unroll=4)
    cross = total[:, BLK:]
    total = total[:, :BLK] + cross + cross.T
    i = lax.broadcasted_iota(jnp.int32, (BLK, BLK), 0)
    j = lax.broadcasted_iota(jnp.int32, (BLK, BLK), 1)
    total = jnp.where(i % 8 == j % 8, total, 0.0)

    pick_rows = (lax.broadcasted_iota(jnp.int32, (REP, BLK), 0)
                 == replicas_of(place, lax.broadcasted_iota(jnp.int32, (REP, BLK), 1) // 8)).astype(F32)
    pick_cols = (lax.broadcasted_iota(jnp.int32, (BLK, 128), 1) % REP
                 == replicas_of(place, lax.broadcasted_iota(jnp.int32, (BLK, 128), 0) // 8)).astype(F32)
    gram = jnp.dot(jnp.dot(pick_rows, total, preferred_element_type=F32, precision=HIGH), pick_cols,
                   preferred_element_type=F32, precision=HIGH)
    lane = lax.broadcasted_iota(jnp.int32, (8, 128), 1)
    packed = jnp.zeros((8, 128), F32)
    for q in range(REP // 8):
        packed = packed + jnp.where(lane // REP == q, gram[8 * q:8 * q + 8], 0.0)
    mean = jnp.sum(weights_ref[...], axis=(0, 1), keepdims=True) / TOK
    means = jnp.where(lane % REP == place[0] * NZ + place[1], mean, 0.0)
    for copy in range(sums_ref.shape[0]):
        sums_ref[copy, 0:8] = packed
        sums_ref[copy, 8:16] = means
    for out in outs:
        out.wait()


def grads_and_sums(place, x_pieces, pieces, weights):
    layout = [(piece.shape, *where) for piece, *where in pieces]
    any_spec = pl.BlockSpec(memory_space=pl.ANY)
    return pl.pallas_call(
        functools.partial(grads_kernel, layout),
        out_shape=(jax.ShapeDtypeStruct((REP, BLK, BLK), F32), jax.ShapeDtypeStruct((NX * NY, 16, 128), F32)),
        in_specs=[pl.BlockSpec(memory_space=pltpu.SMEM)] + [any_spec] * (len(x_pieces) + len(pieces))
        + [pl.BlockSpec(memory_space=pltpu.VMEM)],
        out_specs=(any_spec, pl.BlockSpec(memory_space=pltpu.VMEM)),
        scratch_shapes=[
            pltpu.VMEM((NY, NC, REP, TOK // (NY * NC), BLK), BF16),
            pltpu.VMEM((NZ, NX, TOK, BLK), BF16),
            pltpu.VMEM((REP, BLK, BLK), F32),
            pltpu.SemaphoreType.DMA((NY * NC,)),
            pltpu.SemaphoreType.DMA((len(pieces),)),
            pltpu.SemaphoreType.DMA((NX,)),
        ],
        compiler_params=pltpu.CompilerParams(vmem_limit_bytes=58 * 2**20),
        cost_estimate=pl.CostEstimate(flops=6 * 10**9, bytes_accessed=24 * 2**20, transcendentals=0),
    )(place, *x_pieces, *[piece for piece, *_ in pieces], weights)


def tree_weights(sums):
    lane = lax.broadcasted_iota(jnp.int32, (REP, 128), 1) % REP
    row = lax.broadcasted_iota(jnp.int32, (REP, 128), 0)
    inverse_lanes = float(NY * NC) / sums[8:9]
    inverse_rows = jnp.sum(jnp.where((lax.broadcasted_iota(jnp.int32, (REP, 128), 1) == row),
                                     jnp.broadcast_to(inverse_lanes, (REP, 128)), 0.0), axis=1, keepdims=True)
    wide = lax.broadcasted_iota(jnp.int32, (8, 128), 1)
    table = jnp.concatenate(
        [jnp.where(wide < REP, sums[0:8] if q == 0 else pltpu.roll(sums[0:8], 128 - REP * q, 1), 0.0)
         for q in range(REP // 8)], axis=0)
    table = table + pltpu.roll(table, REP, 1)
    table = table + pltpu.roll(table, 2 * REP, 1)
    table = table * inverse_rows * inverse_lanes
    factor = inverse_rows
    first = lax.broadcasted_iota(jnp.int32, (REP, 128), 1) < REP
    size = REP
    while size > 1:
        half = size // 2
        own = lane == row
        other_rows = lane == (row + half) % REP
        other_lanes = row == (lane + half) % REP
        own_r = jnp.sum(jnp.where(own & first, table, 0.0), axis=1, keepdims=True)
        cross_r = jnp.sum(jnp.where(other_rows & first, table, 0.0), axis=1, keepdims=True)
        own_l = jnp.sum(jnp.where(own, table, 0.0), axis=0, keepdims=True)
        cross_l = jnp.sum(jnp.where(other_lanes, table, 0.0), axis=0, keepdims=True)
        coef_r = 1.0 - cross_r / (2.0 * own_r + EPS_ADA)
        coef_l = 1.0 - cross_l / (2.0 * own_l + EPS_ADA)
        factor = factor * coef_r
        table = table * coef_r * coef_l
        table = table + pltpu.roll(table, half, 0)
        table = table + pltpu.roll(table, half, 1)
        size = half
    return jnp.broadcast_to(factor, (REP, 128))


def update_kernel(place, sums_ref, g_hbm, master_ref, one_ref, two_ref, weights_ref, master_out, one_out, two_out,
                  gv, total, factors, sem):
    group = 4
    copies = [pltpu.make_async_copy(g_hbm.at[pl.ds(r, group)], gv.at[pl.ds(r, group)], sem.at[r])
              for r in range(0, REP, group)]
    for copy in copies:
        copy.start()
    factors[...] = tree_weights(jnp.sum(sums_ref[...], axis=0))

    for no, copy in enumerate(copies):
        scales = []
        for r in range(no * group, (no + 1) * group):
            scale = factors[pl.ds(replica_of(place, r), 1), :]
            scales.append(jnp.concatenate([scale, scale], axis=1))
        copy.wait()

        def strip(s, _):
            at = pl.ds(pl.multiple_of(s * 32, 32), 32)
            part = scales[0] * gv[no * group, at, :]
            for r in range(1, group):
                part = part + scales[r] * gv[no * group + r, at, :]
            total[at, :] = total[at, :] + part if no else part
            return 0

        lax.fori_loop(0, BLK // 32, strip, 0, unroll=8)

    combined = total[...]
    new_one = 0.9 * one_ref[...] + 0.1 * combined
    new_two = 0.95 * two_ref[...] + 0.05 * combined * combined
    first_hat = new_one / (1.0 - 0.9**STEP)
    second_hat = new_two / (1.0 - 0.95**STEP)
    master = master_ref[...]
    updated = master - 0.001 * (first_hat / (jnp.sqrt(second_hat) + 1e-08) + 0.1 * master)
    weights_ref[...] = updated.astype(BF16)
    master_out[...] = updated
    one_out[...] = new_one
    two_out[...] = new_two


def update(place, sums, grads, master, one, two):
    vmem = pl.BlockSpec(memory_space=pltpu.VMEM)
    state = jax.ShapeDtypeStruct((BLK, BLK), F32)
    return pl.pallas_call(
        update_kernel,
        out_shape=(jax.ShapeDtypeStruct((BLK, BLK), BF16), state, state, state),
        in_specs=[pl.BlockSpec(memory_space=pltpu.SMEM), vmem, pl.BlockSpec(memory_space=pl.ANY), vmem, vmem, vmem],
        out_specs=(vmem,) * 4,
        scratch_shapes=[
            pltpu.VMEM((REP, BLK, BLK), F32),
            pltpu.VMEM((BLK, BLK), F32),
            pltpu.VMEM((REP, 128), F32),
            pltpu.SemaphoreType.DMA((REP,)),
        ],
        compiler_params=pltpu.CompilerParams(vmem_limit_bytes=58 * 2**20),
        cost_estimate=pl.CostEstimate(flops=5 * 10**6, bytes_accessed=10 * 2**20, transcendentals=0),
    )(place, sums, grads, master, one, two)


def place_kernel(first, count, place, *refs):
    pieces, out_hbm, held, sem, out_sem = refs[:count], *refs[-4:]
    copies, outs = [], []
    for no in range(count):
        for i in range(2):
            slot = ((first + no) // NX * 2 + i) * NX + no % NX
            at = no * 2 + i
            copies.append(pltpu.make_async_copy(pieces[no].at[i], held.at[at], sem.at[at]))
            outs.append(pltpu.make_async_copy(held.at[at], out_hbm.at[replica_of(place, slot)], out_sem.at[at]))
    for copy in copies:
        copy.start()
    for copy, out in zip(copies, outs):
        copy.wait()
        out.start()
    for out in outs:
        out.wait()


def place_rows(place, pieces, first, out):
    any_spec = pl.BlockSpec(memory_space=pl.ANY)
    count = len(pieces)
    return pl.pallas_call(
        functools.partial(place_kernel, first, count),
        out_shape=jax.ShapeDtypeStruct((REP, BLK, BLK), BF16),
        in_specs=[pl.BlockSpec(memory_space=pltpu.SMEM)] + [any_spec] * (count + len(out)),
        out_specs=any_spec,
        scratch_shapes=[
            pltpu.VMEM((2 * count, BLK, BLK), BF16),
            pltpu.SemaphoreType.DMA((2 * count,)),
            pltpu.SemaphoreType.DMA((2 * count,)),
        ],
        input_output_aliases={1 + count: 0} if out else {},
        compiler_params=pltpu.CompilerParams(vmem_limit_bytes=56 * 2**20),
        cost_estimate=pl.CostEstimate(flops=0, bytes_accessed=2**18 * count, transcendentals=0),
    )(place, *pieces, *out)


def totals_of_groups(sums):
    sums = jnp.sum(lax.all_to_all(sums, ("x", "y"), 0, 0), axis=0)
    return lax.all_to_all(jnp.broadcast_to(sums[None], (NZ * NC,) + sums.shape), ("z", "c"), 0, 0)


def gather_tokens(own):
    ahead, behind = near(own, "y", NY, 1), near(own, "y", NY, -1)
    mine = [own, ahead, behind, near(ahead, "y", NY, -1)]
    return mine + [shift(piece, "c", NC, 1) for piece in mine]


def local(token_rows, advantage, cotangent, master, moment_one, moment_two):
    x, z, y, core = (lax.axis_index(name) for name in ("x", "z", "y", "c"))
    place = jnp.stack([x, z, side(x, core), side(z, core), y, core, side(y, core)]).astype(jnp.int32)
    weights = lax.all_gather(advantage, ("y", "c"), axis=0, tiled=True).astype(F32) * SCALE_FIXED
    weighted = (weights[:, None] * cotangent.astype(F32)).astype(BF16)
    own = lax.all_to_all(token_rows, ("x", "z"), 1, 0, tiled=True).reshape(REP, -1, BLK)
    x_pieces = gather_tokens(own)
    grads, sums = grads_and_sums(place, x_pieces, gather_plane(weighted, ROWS_A, CHUNKS), weights.reshape(-1, 128))
    sums = totals_of_groups(sums)
    new_weights, new_master, new_one, new_two = update(place, sums, grads, master, moment_one, moment_two)
    pieces = [piece[:, 0] for piece, *_ in gather_plane(new_weights, BLK, 4)]
    early = len(pieces) - NX
    out = place_rows(place, pieces[:early], 0, ())
    out = place_rows(place, pieces[early:], early, (out,))
    return (out.reshape(REP * BLK, BLK), new_master, new_one, new_two)


def solution(mesh):
    fine = Mesh(mesh.devices.reshape(NX, NZ, NY, NC), ("x", "z", "y", "c"))
    dp, tensor = ("x", "z"), ("y", "c")
    state = P(dp, tensor)
    return jax.shard_map(
        local,
        mesh=fine,
        in_specs=(P(dp + tensor, None), P(dp + tensor), state, state, state, state),
        out_specs=(P(None, tensor), state, state, state),
        check_vma=False,
    )
```

```python
import functools
import jax
import jax.numpy as jnp
from jax import lax
from jax.experimental import pallas as pl
from jax.experimental.pallas import tpu as pltpu
from jax.sharding import Mesh, PartitionSpec as P

STEP = 10
SCALE_FIXED = 2.0 ** (-12)
EPS_ADA = 1e-06

NX, NZ, NY, NC = 4, 8, 4, 2
REP = NX * NZ
TOK = 512
BLK = 256
ROWS_A = 352
CHUNKS = 2
F32 = jnp.float32
BF16 = jnp.bfloat16
HIGH = lax.Precision.HIGHEST


def shift(array, axis, size, by):
    return lax.ppermute(array, axis, [(i, (i + by) % size) for i in range(size)])


def side(at, core):
    return 1 - 2 * ((at + core) % 2)


def near(array, axis, size, which):
    pairs = [(a * NC + c, (a + which * side(a, c)) % size * NC + c) for a in range(size) for c in range(NC)]
    return lax.ppermute(array, (axis, "c"), pairs)


def swapped_ring(block, axis, size):
    held, which = jnp.stack([block, near(block, axis, size, 1)]), -1
    found = [held]
    for _ in range(size // 2 - 1):
        held = near(held, axis, size, which)
        found.append(held)
        which = -which
    return found


def gather_plane(block, cut, chunks):
    out, kz = [], 0
    lines = swapped_ring(block[:cut], "z", NZ)
    for chunk in range(chunks):
        line = lines[chunk * 4 // chunks:(chunk + 1) * 4 // chunks]
        line = line[0] if len(line) == 1 else jnp.concatenate(line)
        ahead, behind = near(line, "x", NX, 1), near(line, "x", NX, -1)
        for kx, piece in enumerate((line, ahead, behind, near(ahead, "x", NX, -1))):
            out.append((piece[:, None], 0, kz, kx))
        kz += line.shape[0]
    if cut < block.shape[0]:
        for no, piece in enumerate(swapped_ring(jnp.concatenate(swapped_ring(block[cut:], "x", NX)), "z", NZ)):
            out.append((piece, cut, 2 * no, 0))
    return out


STEPS = (0, 1, -1, -2, 2, 3, -3, -4)


def step_of(k):
    return sum(jnp.where(k == i, step, 0) for i, step in enumerate(STEPS))


def replicas_of(place, slots):
    x = lax.rem(place[0] + place[2] * step_of(slots % NX) + NX, NX)
    z = lax.rem(place[1] + place[3] * step_of(slots // NX) + NZ, NZ)
    return x * NZ + z


def replica_of(place, slot):
    x = lax.rem(place[0] + place[2] * STEPS[slot % NX] + NX, NX)
    z = lax.rem(place[1] + place[3] * STEPS[slot // NX] + NZ, NZ)
    return x * NZ + z


def grads_kernel(layout, place, *refs):
    tokens = NY * NC
    x_pieces, refs = refs[:tokens], refs[tokens:]
    count = len(layout)
    pieces, (weights_ref, g_hbm, sums_ref) = refs[:count], refs[count:count + 3]
    xv, wv, gv, xsem, wsem, gsem = refs[count + 3:]
    y, core, turn = place[4], place[5], place[6]
    parts = []
    for no in range(tokens):
        c = core if no < NY else 1 - core
        row = lax.rem(y + (turn if no < NY else -turn) * STEPS[no % NY] + NY, NY)
        parts.append(pltpu.make_async_copy(x_pieces[no], xv.at[row, c], xsem.at[no]))
    loads = []
    for no, ((nz, nx, rows, _), offset, kz, kx) in enumerate(layout):
        loads.append(pltpu.make_async_copy(
            pieces[no], wv.at[pl.ds(kz, nz), pl.ds(kx, nx), pl.ds(offset, rows)], wsem.at[no]))
    for copy in parts + [loads[no] for no in sorted(range(count), key=lambda no: layout[no][2])]:
        copy.start()
    for copy in parts:
        copy.wait()

    def multiply(slot, _):
        rows = xv[:, :, replicas_of(place, slot)].reshape(TOK, BLK)
        gv[slot] = lax.dot_general(rows, wv[slot // NX, lax.rem(slot, NX)], (((0,), (0,)), ((), ())),
                                   preferred_element_type=F32)
        return 0

    outs = []
    waited = set()
    for part in range(NZ // 2):
        for no, (_, _, kz, _) in enumerate(layout):
            if kz < 2 * part + 2 and no not in waited:
                loads[no].wait()
                waited.add(no)
        lax.fori_loop(part * 2 * NX, (part + 1) * 2 * NX, multiply, 0, unroll=8)
        at = pl.ds(part * 2 * NX, 2 * NX)
        outs.append(pltpu.make_async_copy(gv.at[at], g_hbm.at[at], gsem.at[part]))
        outs[-1].start()

    def add(j, total):
        y = jnp.concatenate(
            [gv[:, pl.ds(pl.multiple_of(j * 32 + 8 * h, 8), 8), :].reshape(BLK, BLK) for h in range(4)], axis=1)
        high = y.astype(BF16)
        low = (y - high.astype(F32)).astype(BF16)
        both = jnp.concatenate([high, low], axis=0)
        return total + lax.dot_general(high, both, (((1,), (1,)), ((), ())), preferred_element_type=F32)

    total = lax.fori_loop(0, BLK // 32, add, jnp.zeros((BLK, 2 * BLK), F32), unroll=4)
    cross = total[:, BLK:]
    total = total[:, :BLK] + cross + cross.T
    i = lax.broadcasted_iota(jnp.int32, (BLK, BLK), 0)
    j = lax.broadcasted_iota(jnp.int32, (BLK, BLK), 1)
    total = jnp.where(i % 8 == j % 8, total, 0.0)

    pick_rows = (lax.broadcasted_iota(jnp.int32, (REP, BLK), 0)
                 == replicas_of(place, lax.broadcasted_iota(jnp.int32, (REP, BLK), 1) // 8)).astype(F32)
    pick_cols = (lax.broadcasted_iota(jnp.int32, (BLK, 128), 1) % REP
                 == replicas_of(place, lax.broadcasted_iota(jnp.int32, (BLK, 128), 0) // 8)).astype(F32)
    gram = jnp.dot(jnp.dot(pick_rows, total, preferred_element_type=F32, precision=HIGH), pick_cols,
                   preferred_element_type=F32, precision=HIGH)
    lane = lax.broadcasted_iota(jnp.int32, (8, 128), 1)
    packed = jnp.zeros((8, 128), F32)
    for q in range(REP // 8):
        packed = packed + jnp.where(lane // REP == q, gram[8 * q:8 * q + 8], 0.0)
    mean = jnp.sum(weights_ref[...], axis=(0, 1), keepdims=True) / TOK
    means = jnp.where(lane % REP == place[0] * NZ + place[1], mean, 0.0)
    for copy in range(sums_ref.shape[0]):
        sums_ref[copy, 0:8] = packed
        sums_ref[copy, 8:16] = means
    for out in outs:
        out.wait()


def grads_and_sums(place, x_pieces, pieces, weights):
    layout = [(piece.shape, *where) for piece, *where in pieces]
    any_spec = pl.BlockSpec(memory_space=pl.ANY)
    return pl.pallas_call(
        functools.partial(grads_kernel, layout),
        out_shape=(jax.ShapeDtypeStruct((REP, BLK, BLK), F32), jax.ShapeDtypeStruct((NX * NY, 16, 128), F32)),
        in_specs=[pl.BlockSpec(memory_space=pltpu.SMEM)] + [any_spec] * (len(x_pieces) + len(pieces))
        + [pl.BlockSpec(memory_space=pltpu.VMEM)],
        out_specs=(any_spec, pl.BlockSpec(memory_space=pltpu.VMEM)),
        scratch_shapes=[
            pltpu.VMEM((NY, NC, REP, TOK // (NY * NC), BLK), BF16),
            pltpu.VMEM((NZ, NX, TOK, BLK), BF16),
            pltpu.VMEM((REP, BLK, BLK), F32),
            pltpu.SemaphoreType.DMA((NY * NC,)),
            pltpu.SemaphoreType.DMA((len(pieces),)),
            pltpu.SemaphoreType.DMA((NX,)),
        ],
        compiler_params=pltpu.CompilerParams(vmem_limit_bytes=58 * 2**20),
        cost_estimate=pl.CostEstimate(flops=6 * 10**9, bytes_accessed=24 * 2**20, transcendentals=0),
    )(place, *x_pieces, *[piece for piece, *_ in pieces], weights)


def tree_weights(sums):
    lane = lax.broadcasted_iota(jnp.int32, (REP, 128), 1) % REP
    row = lax.broadcasted_iota(jnp.int32, (REP, 128), 0)
    inverse_lanes = float(NY * NC) / sums[8:9]
    inverse_rows = jnp.sum(jnp.where((lax.broadcasted_iota(jnp.int32, (REP, 128), 1) == row),
                                     jnp.broadcast_to(inverse_lanes, (REP, 128)), 0.0), axis=1, keepdims=True)
    wide = lax.broadcasted_iota(jnp.int32, (8, 128), 1)
    table = jnp.concatenate(
        [jnp.where(wide < REP, sums[0:8] if q == 0 else pltpu.roll(sums[0:8], 128 - REP * q, 1), 0.0)
         for q in range(REP // 8)], axis=0)
    table = table + pltpu.roll(table, REP, 1)
    table = table + pltpu.roll(table, 2 * REP, 1)
    table = table * inverse_rows * inverse_lanes
    factor = inverse_rows
    first = lax.broadcasted_iota(jnp.int32, (REP, 128), 1) < REP
    size = REP
    while size > 1:
        half = size // 2
        own = lane == row
        other_rows = lane == (row + half) % REP
        other_lanes = row == (lane + half) % REP
        own_r = jnp.sum(jnp.where(own & first, table, 0.0), axis=1, keepdims=True)
        cross_r = jnp.sum(jnp.where(other_rows & first, table, 0.0), axis=1, keepdims=True)
        own_l = jnp.sum(jnp.where(own, table, 0.0), axis=0, keepdims=True)
        cross_l = jnp.sum(jnp.where(other_lanes, table, 0.0), axis=0, keepdims=True)
        coef_r = 1.0 - cross_r / (2.0 * own_r + EPS_ADA)
        coef_l = 1.0 - cross_l / (2.0 * own_l + EPS_ADA)
        factor = factor * coef_r
        table = table * coef_r * coef_l
        table = table + pltpu.roll(table, half, 0)
        table = table + pltpu.roll(table, half, 1)
        size = half
    return jnp.broadcast_to(factor, (REP, 128))


def update_kernel(place, sums_ref, g_hbm, master_ref, one_ref, two_ref, weights_ref, master_out, one_out, two_out,
                  gv, total, factors, sem):
    group = 4
    copies = [pltpu.make_async_copy(g_hbm.at[pl.ds(r, group)], gv.at[pl.ds(r, group)], sem.at[r])
              for r in range(0, REP, group)]
    for copy in copies:
        copy.start()
    factors[...] = tree_weights(jnp.sum(sums_ref[...], axis=0))

    for no, copy in enumerate(copies):
        scales = []
        for r in range(no * group, (no + 1) * group):
            scale = factors[pl.ds(replica_of(place, r), 1), :]
            scales.append(jnp.concatenate([scale, scale], axis=1))
        copy.wait()

        def strip(s, _):
            at = pl.ds(pl.multiple_of(s * 32, 32), 32)
            part = scales[0] * gv[no * group, at, :]
            for r in range(1, group):
                part = part + scales[r] * gv[no * group + r, at, :]
            total[at, :] = total[at, :] + part if no else part
            return 0

        lax.fori_loop(0, BLK // 32, strip, 0, unroll=8)

    combined = total[...]
    new_one = 0.9 * one_ref[...] + 0.1 * combined
    new_two = 0.95 * two_ref[...] + 0.05 * combined * combined
    first_hat = new_one / (1.0 - 0.9**STEP)
    second_hat = new_two / (1.0 - 0.95**STEP)
    master = master_ref[...]
    updated = master - 0.001 * (first_hat / (jnp.sqrt(second_hat) + 1e-08) + 0.1 * master)
    weights_ref[...] = updated.astype(BF16)
    master_out[...] = updated
    one_out[...] = new_one
    two_out[...] = new_two


def update(place, sums, grads, master, one, two):
    vmem = pl.BlockSpec(memory_space=pltpu.VMEM)
    state = jax.ShapeDtypeStruct((BLK, BLK), F32)
    return pl.pallas_call(
        update_kernel,
        out_shape=(jax.ShapeDtypeStruct((BLK, BLK), BF16), state, state, state),
        in_specs=[pl.BlockSpec(memory_space=pltpu.SMEM), vmem, pl.BlockSpec(memory_space=pl.ANY), vmem, vmem, vmem],
        out_specs=(vmem,) * 4,
        scratch_shapes=[
            pltpu.VMEM((REP, BLK, BLK), F32),
            pltpu.VMEM((BLK, BLK), F32),
            pltpu.VMEM((REP, 128), F32),
            pltpu.SemaphoreType.DMA((REP,)),
        ],
        compiler_params=pltpu.CompilerParams(vmem_limit_bytes=58 * 2**20),
        cost_estimate=pl.CostEstimate(flops=5 * 10**6, bytes_accessed=10 * 2**20, transcendentals=0),
    )(place, sums, grads, master, one, two)


def place_kernel(first, count, place, *refs):
    pieces, out_hbm, held, sem, out_sem = refs[:count], *refs[-4:]
    copies, outs = [], []
    for no in range(count):
        for i in range(2):
            slot = ((first + no) // NX * 2 + i) * NX + no % NX
            at = no * 2 + i
            copies.append(pltpu.make_async_copy(pieces[no].at[i], held.at[at], sem.at[at]))
            outs.append(pltpu.make_async_copy(held.at[at], out_hbm.at[replica_of(place, slot)], out_sem.at[at]))
    for copy in copies:
        copy.start()
    for copy, out in zip(copies, outs):
        copy.wait()
        out.start()
    for out in outs:
        out.wait()


def place_rows(place, pieces, first, out):
    any_spec = pl.BlockSpec(memory_space=pl.ANY)
    count = len(pieces)
    return pl.pallas_call(
        functools.partial(place_kernel, first, count),
        out_shape=jax.ShapeDtypeStruct((REP, BLK, BLK), BF16),
        in_specs=[pl.BlockSpec(memory_space=pltpu.SMEM)] + [any_spec] * (count + len(out)),
        out_specs=any_spec,
        scratch_shapes=[
            pltpu.VMEM((2 * count, BLK, BLK), BF16),
            pltpu.SemaphoreType.DMA((2 * count,)),
            pltpu.SemaphoreType.DMA((2 * count,)),
        ],
        input_output_aliases={1 + count: 0} if out else {},
        compiler_params=pltpu.CompilerParams(vmem_limit_bytes=56 * 2**20),
        cost_estimate=pl.CostEstimate(flops=0, bytes_accessed=2**18 * count, transcendentals=0),
    )(place, *pieces, *out)


def totals_of_groups(sums):
    sums = jnp.sum(lax.all_to_all(sums, ("x", "y"), 0, 0), axis=0)
    return lax.all_to_all(jnp.broadcast_to(sums[None], (NZ * NC,) + sums.shape), ("z", "c"), 0, 0)


def gather_tokens(own):
    ahead, behind = near(own, "y", NY, 1), near(own, "y", NY, -1)
    mine = [own, ahead, behind, near(ahead, "y", NY, -1)]
    return mine + [shift(piece, "c", NC, 1) for piece in mine]


def local(token_rows, advantage, cotangent, master, moment_one, moment_two):
    x, z, y, core = (lax.axis_index(name) for name in ("x", "z", "y", "c"))
    place = jnp.stack([x, z, side(x, core), side(z, core), y, core, side(y, core)]).astype(jnp.int32)
    weights = lax.all_gather(advantage, ("y", "c"), axis=0, tiled=True).astype(F32) * SCALE_FIXED
    weighted = (weights[:, None] * cotangent.astype(F32)).astype(BF16)
    own = lax.all_to_all(token_rows, ("x", "z"), 1, 0, tiled=True).reshape(REP, -1, BLK)
    x_pieces = gather_tokens(own)
    grads, sums = grads_and_sums(place, x_pieces, gather_plane(weighted, ROWS_A, CHUNKS), weights.reshape(-1, 128))
    sums = totals_of_groups(sums)
    new_weights, new_master, new_one, new_two = update(place, sums, grads, master, moment_one, moment_two)
    pieces = [piece[:, 0] for piece, *_ in gather_plane(new_weights, BLK, 4)]
    early = len(pieces) - NX
    out = place_rows(place, pieces[:early], 0, ())
    out = place_rows(place, pieces[early:], early, (out,))
    return (out.reshape(REP * BLK, BLK), new_master, new_one, new_two)


def solution(mesh):
    fine = Mesh(mesh.devices.reshape(NX, NZ, NY, NC), ("x", "z", "y", "c"))
    dp, tensor = ("x", "z"), ("y", "c")
    state = P(dp, tensor)
    return jax.shard_map(
        local,
        mesh=fine,
        in_specs=(P(dp + tensor, None), P(dp + tensor), state, state, state, state),
        out_specs=(P(None, tensor), state, state, state),
        check_vma=False,
    )
```
